256 devices in a mesh: dp: 8 (over x, y_lo), expert: 32 (over y_hi, z, core).
Axes of the slice: x: 4, y: 4 (y_hi: 2, y_lo: 2; y = y_hi * 2 + y_lo), z: 8, core: 2. Of those that a mesh axis runs over, the one named last changes fastest.
Arguments:
- tokens: bfloat16 [2, 16384, 2048], P(None, ('dp', 'expert')), may hold values from -6 to 6
- route_ids: int32 [2, 16384, 10], P(None, ('dp', 'expert')), may hold values from 0 to 63, all different within a row; in each aligned block of 64 rows (0 to 63, 64 to 127, ..., all dimensions but the last counted through in order) at most 12 rows name the same one
- route_gates: float32 [2, 16384, 10], P(None, ('dp', 'expert')), may hold values from 0.1 to 1
- expert_in: bfloat16 [32, 2, 2048, 1024], P('expert', None, 'dp'), may hold values from -0.125 to 0.125
- expert_out: bfloat16 [32, 2, 512, 2048], P('expert', None, None, 'dp'), may hold values from -0.25 to 0.25
- old_plan: int32 [32], replicated, may hold values from 0 to 31, each once
- new_plan: int32 [32], replicated, may hold values from 0 to 31, each once
Outputs:
- mixed: bfloat16 [2, 16384, 2048], P(None, ('dp', 'expert'))
- moved_in: bfloat16 [32, 2048, 1024], P('expert', 'dp')
- moved_out: bfloat16 [32, 512, 2048], P('expert', None, 'dp')
The draws below stay inside these ranges and needn't reach their ends.
Inputs may be any that keep to these rules, and one draw needn't show every extreme that they name: `route_ids`: each token names 10 different experts. In each micro-batch the 64 tokens of one device name no expert in more than 12 of their routes, and some expert in exactly 12. `old_plan`: each movable expert is held by exactly one slot. `new_plan`: each movable expert is held by exactly one slot.
All inputs are finite; a program needn't handle non-finite values.
Results may differ from the reference program's by a relative error of at most 0.0057.
Values may be sent and summed in bfloat16 or wider, within the bound.
A program may use at most 128 MiB of HBM per device.

```python
import math
import jax
import jax.numpy as jnp
import numpy as np
from jax import lax

D = 2048
F = 512
TOPK = 10
MB = 2
TOK_MB = 64
MOVABLE = 32
EXPERTS = 64
TOKENS = 16384
CAP = 12
N_DP = 8
N_EXPERT = 32


def block_scale(rng, extent, shards, smallest, largest):
    factor_of, own = 1.0, jax.random.fold_in(rng, 6)
    for dim, blocks in shards:
        steps = jnp.exp(jax.random.uniform(jax.random.fold_in(own, dim), (blocks,), jnp.float32, smallest / len(shards), largest / len(shards)))
        factor_of = factor_of * jnp.repeat(steps, extent[dim] // blocks).reshape([-1 if axis == dim else 1 for axis in range(len(extent))])
    return factor_of


def routed_block(stream_key, own, number, rows, count, top, limit, slope):
    ranking = jax.random.permutation(stream_key, count)
    crowded, usual = portions_of(count, rows * top, limit, slope, True), portions_of(count, rows * top, limit, slope, False)
    places = jnp.arange(count)

    def named(tallies, turn):
        used = int((tallies > 0).sum())
        fixed = max(1, used // 4)
        moved = fixed + (places - fixed + turn * (used - fixed)) % max(1, count - fixed)
        return jnp.zeros((count,), jnp.int32).at[ranking[jnp.where(places < fixed, places, moved)]].set(jnp.asarray(tallies, jnp.int32))

    tallies = jnp.where(number % 4 == 0, named(crowded, number // 4), named(usual, number - number // 4 - 1))
    mixed = jax.random.permutation(jax.random.fold_in(own, 3), count)
    source_of, sink = mixed[0:count // 2 * 2:2], mixed[1:count // 2 * 2:2]
    margin = jnp.minimum(tallies[source_of] - 1, limit - tallies[sink]) // 2
    margin = jnp.where((source_of == ranking[0]) | (sink == ranking[0]) | (tallies[sink] == 0), 0, jnp.maximum(margin, 0))
    moved = jax.random.randint(jax.random.fold_in(own, 4), (count // 2,), 0, 1 << 20) % (margin + 1)
    tallies = tallies.at[source_of].add(-moved).at[sink].add(moved)
    members = jnp.searchsorted(jnp.cumsum(tallies), jnp.arange(rows * top), side="right").astype(jnp.int32)
    grid = members.reshape(top, rows).T
    grid = grid[jax.random.permutation(jax.random.fold_in(own, 1), rows)]
    turn = jax.random.randint(jax.random.fold_in(own, 2), (rows, 1), 0, top)
    return jnp.take_along_axis(grid, (jnp.arange(top)[None, :] + turn) % top, axis=1)


def portions_of(count, total, most, skew, full):
    portions = [(1 << 20) // math.isqrt(rank ** skew) + 1 for rank in range(1, count + 1)]
    largest = most if full else min(most, max(-(-total // count), total * portions[0] // sum(portions)))
    least = 1 if total - largest >= count - 1 else 0
    holding, surplus = [largest] + [least] * (count - 1), total - largest - least * (count - 1)
    while surplus > 0:
        candidates = [i for i in range(1, count) if holding[i] < largest] or [i for i in range(1, count) if holding[i] < most]
        pool, remaining = sum([portions[i] for i in candidates]), surplus
        for i in candidates:
            more = min(most - holding[i], max(1, remaining * portions[i] // pool), surplus)
            holding[i] = holding[i] + more
            surplus = surplus - more
    return np.array(holding)


def scatter_about(key, shape, deviation, reach, split=(), held_as=jnp.bfloat16):
    loudness = block_scale(key, shape, split, -0.22, 0.18) if split else 1.0
    values = jax.random.normal(key, shape, jnp.float32) * deviation * loudness
    return jnp.minimum(jnp.maximum(values, -reach), reach).astype(held_as)


def setup_inputs(seed: int = 0) -> dict:
    streams_of = jax.random.split(jax.random.key(seed), 8)
    tokens = scatter_about(streams_of[0], (MB, TOKENS, D), 1.0, 6.0, ((1, 256),))
    route_ids_keys = jax.random.split(jax.random.fold_in(streams_of[1], 1), MB * TOKENS // TOK_MB)
    route_ids_turns = jax.random.permutation(jax.random.fold_in(streams_of[1], 3), MB * TOKENS // TOK_MB)
    route_ids = jax.vmap(lambda own, number: routed_block(jax.random.fold_in(streams_of[1], 2), own, number, TOK_MB, EXPERTS, TOPK, CAP, 2))(route_ids_keys, route_ids_turns).reshape((MB, TOKENS, TOPK))
    route_gates = jnp.clip(jnp.exp(math.log(1.0) - 2.3025851 * jax.random.uniform(streams_of[2], (MB, TOKENS, TOPK), jnp.float32) ** block_scale(streams_of[2], (MB, TOKENS, TOPK), ((1, 256),), -0.2, 0.2)), 0.1, 1.0)
    expert_in = scatter_about(streams_of[3], (MOVABLE, 2, D, 2 * F), D ** -0.5, 0.125, ((0, 32), (2, 8)))
    expert_out = scatter_about(streams_of[4], (MOVABLE, 2, F, D), F ** -0.5, 0.25, ((0, 32), (3, 8)))
    old_plan = jax.random.permutation(streams_of[5], MOVABLE).astype(jnp.int32)
    new_plan = jax.random.permutation(streams_of[6], MOVABLE).astype(jnp.int32)
    return dict(tokens=tokens, route_ids=route_ids, route_gates=route_gates, expert_in=expert_in, expert_out=expert_out, old_plan=old_plan, new_plan=new_plan)


def expert_apply(picked, weight_in, weight_out):
    hidden_units = weight_out.shape[0]
    projected = jnp.dot(picked, weight_in, preferred_element_type=jnp.float32)
    hidden = (jax.nn.silu(projected[:, :hidden_units]) * projected[:, hidden_units:]).astype(jnp.bfloat16)
    return jnp.dot(hidden, weight_out, preferred_element_type=jnp.float32).astype(jnp.bfloat16)


def reference(tokens, route_ids, route_gates, expert_in, expert_out, old_plan, new_plan):
    inverse_old = jnp.zeros((MOVABLE,), jnp.int32).at[old_plan].set(jnp.arange(MOVABLE, dtype=jnp.int32))
    source = inverse_old[new_plan]
    moved_in = expert_in[source, 1]
    moved_out = expert_out[source, 1]
    owners = jnp.concatenate([jnp.arange(MOVABLE, dtype=jnp.int32), inverse_old])
    slot_of = jnp.concatenate([jnp.zeros((MOVABLE,), jnp.int32), jnp.ones((MOVABLE,), jnp.int32)])
    bound = N_DP * N_EXPERT * CAP
    total = TOKENS * TOPK
    outputs = []
    for batch_index in range(MB):
        flat = route_ids[batch_index].reshape(-1)
        order = jnp.argsort(flat, stable=True).astype(jnp.int32)
        ordered = flat[order]
        labels = jnp.arange(EXPERTS, dtype=jnp.int32)
        starts = jnp.searchsorted(ordered, labels, side="left").astype(jnp.int32)
        ends = jnp.searchsorted(ordered, labels, side="right").astype(jnp.int32)
        gates_flat = route_gates[batch_index].reshape(-1)
        batch_tokens = tokens[batch_index]

        def add_expert(carry, expert):
            offsets = jnp.arange(bound, dtype=jnp.int32)
            valid = offsets < ends[expert] - starts[expert]
            route = order[jnp.clip(starts[expert] + offsets, 0, total - 1)]
            token_rows = route // TOPK
            weight_in = expert_in[owners[expert], slot_of[expert]]
            weight_out = expert_out[owners[expert], slot_of[expert]]
            result = expert_apply(batch_tokens[token_rows], weight_in, weight_out)
            scale = jnp.where(valid, gates_flat[route], jnp.zeros_like(gates_flat[route]))
            return carry.at[token_rows].add(scale[:, None] * result.astype(jnp.float32)), None

        summed, unused = lax.scan(add_expert, jnp.zeros((TOKENS, D), jnp.float32), jnp.arange(EXPERTS, dtype=jnp.int32))
        outputs.append(summed.astype(jnp.bfloat16))
    return jnp.stack(outputs), moved_in, moved_out
```

```python
import jax
import jax.numpy as jnp
from jax import lax
from jax.experimental import pallas as pl
from jax.experimental.pallas import tpu as pltpu
from jax.sharding import PartitionSpec as P

MESH = pl.DeviceIdType.MESH
NX, NYL, NYH, NZ, NC = 4, 2, 2, 8, 2
NDP, NEX = NX * NYL, NYH * NZ * NC
MB, TOK, D, F, TOPK, CAP = 2, 64, 2048, 512, 10, 12
DK = D // NDP
GRP = NYH * NC * TOK
ROWS = NYH * NC * CAP
WIDE = D + 128
NB = 512
BF, F32 = jnp.bfloat16, jnp.float32


def kernel(
    tokens, meta, expert_in, expert_out, plan, source,
    mixed, moved_in, moved_out,
    T, WI, WO, XY, H, GT, DD, RV, YS, YR, OWN, Q0, Q1, Q2, Q3,
    ld_sem, agr_s, agr_r, agy_s, agy_r, ags_s, ags_r,
    w1x_s, w1x_r, w1y_s, w1y_r, w0y_s, w0y_r, w0x_s, w0x_r,
    sib_s, sib_r, rs_s, rs_r, rsy_s, rsy_r, q1_s, q1_r, q2_s, q2_r,
):
    dp, ex = lax.axis_index("dp"), lax.axis_index("expert")
    x, yl = dp // NYL, dp % NYL
    yh, z, c = ex // (NZ * NC), (ex // NC) % NZ, ex % NC

    def zat(d):
        return (z + d + NZ) % NZ

    def xat(d):
        return ((x + d + NX) % NX) * NYL + yl

    def at_z(d):
        return (dp, (yh * NZ + zat(d)) * NC + c)

    def at_x(d):
        return (xat(d), ex)

    ypart = (dp, ((1 - yh) * NZ + z) * NC + c)
    sibling = (dp, (yh * NZ + z) * NC + 1 - c)
    lpart = (x * NYL + 1 - yl, ex)

    def remote(src, dst, ss, rs, dev):
        return pltpu.make_async_remote_copy(
            src_ref=src, dst_ref=dst, send_sem=ss, recv_sem=rs,
            device_id=dev, device_id_type=MESH,
        )

    sent = {}

    def go(key, cp):
        cp.start()
        sent.setdefault(key, []).append(cp)

    def drain(key):
        for cp in sent.pop(key, []):
            cp.wait_send()

    loads_t = []
    for mb in range(MB):
        loads_t.append((
            pltpu.make_async_copy(tokens.at[mb], T.at[mb, z, yh, c, :, pl.ds(0, D)], ld_sem.at[2 * mb]),
            pltpu.make_async_copy(meta.at[mb], T.at[mb, z, yh, c, :, pl.ds(D, 128)], ld_sem.at[2 * mb + 1]),
        ))
    loads_w = []
    for s in range(2):
        loads_w.append(pltpu.make_async_copy(expert_in.at[0, s], WI.at[s, dp], ld_sem.at[4 + 2 * s]))
        loads_w.append(pltpu.make_async_copy(expert_out.at[0, s], WO.at[s, dp], ld_sem.at[5 + 2 * s]))
    for pair in loads_t:
        for cp in pair:
            cp.start()
    for cp in loads_w:
        cp.start()

    barrier = pltpu.get_barrier_semaphore()

    @pl.loop(1, NEX)
    def _(i):
        pl.semaphore_signal(barrier, inc=1, device_id=(dp, (ex + i) % NEX), device_id_type=MESH)

    for dev in (at_x(1), at_x(-1), lpart):
        pl.semaphore_signal(barrier, inc=1, device_id=dev, device_id_type=MESH)
    pl.semaphore_wait(barrier, NEX - 1 + 3)

    sib_count = [0, 0]

    def chunk(mb, zs, ys):
        return T.at[mb, zs, ys, c]

    def to_sibling(mb, zs, ys):
        k = sib_count[mb]
        sib_count[mb] += 1
        go(("ag", mb), remote(chunk(mb, zs, ys), chunk(mb, zs, ys), ags_s.at[mb, k], ags_r.at[mb, k], sibling))

    def wait_sibling(mb):
        for k in range(NYH * NZ):
            ref = T.at[mb, 0, 0, 0]
            remote(ref, ref, ags_s.at[mb, k], ags_r.at[mb, k], sibling).wait_recv()

    def ring(mb, sgn, d, rel):
        dr = 0 if sgn > 0 else 1
        if d == 3:
            ys = dr
        else:
            ys = yh if rel == 0 else 1 - yh
        ref = chunk(mb, zat(-sgn * d), ys)
        go(("ag", mb), remote(ref, ref, agr_s.at[mb, dr, d, rel], agr_r.at[mb, dr, d, rel], at_z(sgn)))

    def ring_wait(mb, sgn, d, rel):
        dr = 0 if sgn > 0 else 1
        if d == 4:
            ys = dr
        else:
            ys = yh if rel == 0 else 1 - yh
        zs = zat(-sgn * d)
        ref = chunk(mb, zs, ys)
        remote(ref, ref, agr_s.at[mb, dr, d - 1, rel], agr_r.at[mb, dr, d - 1, rel], at_z(sgn)).wait_recv()
        to_sibling(mb, zs, ys)

    def ag_y(mb):
        ref = chunk(mb, z, yh)
        go(("ag", mb), remote(ref, ref, agy_s.at[mb], agy_r.at[mb], ypart))

    def ag_own(mb):
        for sgn in (1, -1):
            ring(mb, sgn, 0, 0)
        to_sibling(mb, z, yh)

    def ag_partner(mb):
        ref = chunk(mb, z, 1 - yh)
        remote(ref, ref, agy_s.at[mb], agy_r.at[mb], ypart).wait_recv()
        for sgn in (1, -1):
            ring(mb, sgn, 0, 1)
        to_sibling(mb, z, 1 - yh)

    def ag_step(mb, d):
        for rel in (0, 1):
            for sgn in (1, -1):
                if d == 4 and rel == 1:
                    continue
                ring_wait(mb, sgn, d, rel)
                if d < 3:
                    ring(mb, sgn, d, rel)
        if d == 3:
            for sgn in (1, -1):
                ring(mb, sgn, 3, 0)

    def wblk(s, b, io, half=None):
        ref = WI if io == 0 else WO
        if half is None:
            return ref.at[s, b]
        rows = (DK if io == 0 else F) // 2
        return ref.at[s, b, pl.ds(half * rows, rows)]

    def wcopy(s, b, io, half, ss, rs, dev):
        ref = wblk(s, b, io, half)
        return remote(ref, ref, ss, rs, dev)

    def w1x(sgn, d):
        dr = 0 if sgn > 0 else 1
        for io in (0, 1):
            half = None if d == 0 else dr
            go("w", wcopy(1, xat(-sgn * d), io, half, w1x_s.at[dr, d, io], w1x_r.at[dr, d, io], at_x(sgn)))

    def w1x_wait(sgn, d):
        dr = 0 if sgn > 0 else 1
        for io in (0, 1):
            half = None if d == 1 else dr
            wcopy(1, xat(-sgn * d), io, half, w1x_s.at[dr, d - 1, io], w1x_r.at[dr, d - 1, io], at_x(sgn)).wait_recv()

    def w1y(k):
        d = (0, 1, -1, 2)[k]
        for io in (0, 1):
            go("w", wcopy(1, xat(d), io, None, w1y_s.at[k, io], w1y_r.at[k, io], lpart))

    def w1y_wait(k):
        d = (0, 1, -1, 2)[k]
        for io in (0, 1):
            b = ((x + d + NX) % NX) * NYL + 1 - yl
            wcopy(1, b, io, None, w1y_s.at[k, io], w1y_r.at[k, io], lpart).wait_recv()

    def w0y():
        for io in (0, 1):
            go("w", wcopy(0, dp, io, None, w0y_s.at[io], w0y_r.at[io], lpart))

    def w0y_wait():
        for io in (0, 1):
            wcopy(0, x * NYL + 1 - yl, io, None, w0y_s.at[io], w0y_r.at[io], lpart).wait_recv()

    def w0blk(d, rel):
        return ((x + d + NX) % NX) * NYL + (yl if rel == 0 else 1 - yl)

    def w0x(sgn, d, rel):
        dr = 0 if sgn > 0 else 1
        for io in (0, 1):
            half = None if d == 0 else dr
            go("w", wcopy(0, w0blk(-sgn * d, rel), io, half, w0x_s.at[dr, d, rel, io], w0x_r.at[dr, d, rel, io], at_x(sgn)))

    def w0x_wait(sgn, d, rel):
        dr = 0 if sgn > 0 else 1
        for io in (0, 1):
            half = None if d == 1 else dr
            wcopy(0, w0blk(-sgn * d, rel), io, half, w0x_s.at[dr, d - 1, rel, io], w0x_r.at[dr, d - 1, rel, io], at_x(sgn)).wait_recv()

    def pack():
        @pl.loop(0, NEX // 2)
        def _(i):
            for h in range(2):
                j = 2 * i + h
                Q0[j, :, 0:512] = WI[1, dp, pl.ds(pl.multiple_of(i * 16, 16), 16), h * 512:(h + 1) * 512]
                Q0[j, :, 512:768] = WO[1, dp, pl.ds(pl.multiple_of(j * 16, 16), 16), :]
        Q1[ex] = Q0[ex]

    def spread(src, dst, ss, rs):
        @pl.loop(1, NEX)
        def _(i):
            j = (ex + i) % NEX
            remote(src.at[j], dst.at[ex], ss.at[i], rs.at[i], (dp, j)).start()

    def spread_wait(src, dst, ss, rs):
        @pl.loop(1, NEX)
        def _(i):
            j = (ex - i + NEX) % NEX
            remote(src.at[j], dst.at[j], ss.at[i], rs.at[i], (dp, j)).wait_recv()

    def spread_drain(src, dst, ss, rs):
        @pl.loop(1, NEX)
        def _(i):
            j = (ex + i) % NEX
            remote(src.at[j], dst.at[ex], ss.at[i], rs.at[i], (dp, j)).wait_send()

    def sort():
        @pl.loop(0, NEX)
        def _(s):
            Q2[s] = Q1[source[s]]
        Q3[ex] = Q2[ex]

    def unpack():
        @pl.loop(0, NEX // 2)
        def _(i):
            for h in range(2):
                j = 2 * i + h
                moved_in[0, pl.ds(pl.multiple_of(i * 16, 16), 16), h * 512:(h + 1) * 512] = Q3[j, :, 0:512]
                moved_out[0, pl.ds(pl.multiple_of(j * 16, 16), 16), :] = Q3[j, :, 512:768]

    def pick(mb):
        @pl.loop(0, NZ)
        def _(g):
            info = T[mb, g, :, :, :, D:WIDE].reshape(GRP, 128).astype(F32).T
            ids, hi, lo = info[0:16], info[16:32], info[32:48]
            names = (ex.astype(F32), (NEX + plan[ex]).astype(F32))
            masks, his, los = [], [], []
            for name in names:
                hit = ids == name
                masks.append(jnp.max(jnp.where(hit, 1.0, 0.0), axis=0, keepdims=True))
                his.append(jnp.sum(jnp.where(hit, hi, 0.0), axis=0, keepdims=True))
                los.append(jnp.sum(jnp.where(hit, lo, 0.0), axis=0, keepdims=True))
            row = lax.broadcasted_iota(jnp.int32, (16, GRP), 0)
            stacked = jnp.where(row == 0, masks[0], jnp.where(row == 1, masks[1], 0.0))
            a = lax.broadcasted_iota(jnp.int32, (GRP, GRP), 0)
            b = lax.broadcasted_iota(jnp.int32, (GRP, GRP), 1)
            before = jnp.where((a // TOK == b // TOK) & (a < b), 1.0, 0.0).astype(BF)
            rank = jnp.dot(stacked.astype(BF), before, preferred_element_type=F32)
            lane = lax.broadcasted_iota(jnp.int32, (1, GRP), 1)
            first = ((lane // TOK) * CAP).astype(F32)
            place = lax.broadcasted_iota(jnp.int32, (ROWS, GRP), 0).astype(F32)
            hot, his_, los_ = [], [], []
            for s in range(2):
                key = jnp.where(masks[s] > 0.0, rank[s:s + 1] + first, -1.0)
                at = place == key
                hot.append(jnp.where(at, 1.0, 0.0))
                his_.append(jnp.where(at, his[s], 0.0))
                los_.append(jnp.where(at, los[s], 0.0))
            back = jnp.concatenate(his_ + los_ + [jnp.zeros((256 - 4 * ROWS, GRP), F32)], axis=0).T
            GT[mb, g] = back.astype(BF).reshape(NYH, NC, TOK, 256)
            pickm = jnp.concatenate(hot, axis=0).astype(BF)
            for n in range(D // NB):
                cols = pl.ds(n * NB, NB)
                tok = T[mb, g, :, :, :, cols].reshape(GRP, NB)
                got = jnp.dot(pickm, tok, preferred_element_type=F32).astype(BF)
                XY[mb, g, :, :, cols] = got.reshape(2, ROWS, NB)

    def ffn(mb, s):
        @pl.loop(0, F // 256)
        def _(n):
            xs = XY[mb, :, s].reshape(NZ * ROWS, D)
            col = pl.multiple_of(n * 256, 256)
            gate = jnp.dot(xs, WI[s, :, :, pl.ds(col, 256)].reshape(D, 256), preferred_element_type=F32)
            up = jnp.dot(xs, WI[s, :, :, pl.ds(col + F, 256)].reshape(D, 256), preferred_element_type=F32)
            H[:, pl.ds(col, 256)] = (gate / (1.0 + jnp.exp(-gate)) * up).astype(BF)

        @pl.loop(0, NDP)
        def _(b):
            y = jnp.dot(H[...], WO[s, b], preferred_element_type=F32).astype(BF)
            XY[mb, :, s, :, pl.ds(pl.multiple_of(b * DK, DK), DK)] = y.reshape(NZ, ROWS, DK)

    def part(mb, zd, core, n):
        cols = pl.ds(pl.multiple_of(n * NB, NB), NB)
        g = GT[mb, zd, :, core].reshape(NYH * TOK, 256)
        y = XY[mb, zd, :, :, cols].reshape(2 * ROWS, NB)
        both = jnp.concatenate([y, y, jnp.zeros((256 - 4 * ROWS, NB), BF)], axis=0)
        return jnp.dot(g, both, preferred_element_type=F32).reshape(NYH, TOK, NB)

    def dref(mb, zd, y, cols=pl.ds(0, D)):
        if mb == 0:
            return DD.at[zd, y, :, cols]
        return T.at[0, zd, y, 0, :, cols]

    def sref(mb, zd, y, cols=pl.ds(0, D)):
        return T.at[mb, zd, y, 1, :, cols]

    def to_sib(mb):
        @pl.loop(0, NZ)
        def _(i):
            mag = 4 - (i + 1) // 2
            zd = zat((2 * (i % 2) - 1) * mag)

            @pl.loop(0, D // NB)
            def _(n):
                cols = pl.ds(pl.multiple_of(n * NB, NB), NB)
                v = part(mb, zd, 1 - c, n).astype(BF)
                for y in range(NYH):
                    sref(mb, zd, y, cols)[...] = v[y]

            for y in range(NYH):
                remote(sref(mb, zd, y), dref(mb, zd, y), sib_s.at[mb, i, y], sib_r.at[mb, i, y], sibling).start()

    def to_sib_drain(mb):
        @pl.loop(0, NZ)
        def _(i):
            mag = 4 - (i + 1) // 2
            zd = zat((2 * (i % 2) - 1) * mag)
            for y in range(NYH):
                remote(sref(mb, zd, y), dref(mb, zd, y), sib_s.at[mb, i, y], sib_r.at[mb, i, y], sibling).wait_send()

    def rs_copy(mb, dr, k, y, zd):
        sgn = 1 if dr == 0 else -1
        return remote(dref(mb, zd, y), RV.at[mb, dr, k, y], rs_s.at[mb, dr, k, y], rs_r.at[mb, dr, k, y], at_z(sgn))

    def rs_step(mb, j):
        for dr in ((0,) if j in (4, 0) else (0, 1)):
            sgn = 1 if dr == 0 else -1
            zd = zat(sgn * j)
            i = 0 if j == 4 else 7 if j == 0 else 2 * (4 - j) - (1 if dr == 0 else 0)
            for y in range(NYH):
                remote(sref(mb, zd, y), dref(mb, zd, y), sib_s.at[mb, i, y], sib_r.at[mb, i, y], sibling).wait_recv()
            arrived = []
            if j < 4:
                for arm in ((0, 1) if j == 0 else (dr,)):
                    for y in ((arm,) if j == 3 else (0, 1)):
                        rs_copy(mb, arm, 3 - j, y, zd).wait_recv()
                        arrived.append((arm, y))

            @pl.loop(0, D // NB)
            def _(n):
                cols = pl.ds(pl.multiple_of(n * NB, NB), NB)
                v = part(mb, zd, c, n)
                for y in range(NYH):
                    acc = v[y] + dref(mb, zd, y, cols)[...].astype(F32)
                    for arm, ya in arrived:
                        if ya == y:
                            acc = acc + RV[mb, arm, 3 - j, y, :, cols].astype(F32)
                    if j == 0:
                        OWN[mb, y, :, cols] = acc
                    else:
                        dref(mb, zd, y, cols)[...] = acc.astype(BF)

            if j == 4:
                go("rs", rs_copy(mb, 0, 0, 0, zd))
                go("rs", rs_copy(mb, 1, 0, 1, zd))
            elif j > 0:
                for y in range(NYH):
                    go("rs", rs_copy(mb, dr, 4 - j, y, zd))
            else:
                YS[mb] = OWN[mb, 1 - yh].astype(BF)
                go("rs", remote(YS.at[mb], YR.at[mb], rsy_s.at[mb], rsy_r.at[mb], ypart))

    def rs_end(mb):
        remote(YS.at[mb], YR.at[mb], rsy_s.at[mb], rsy_r.at[mb], ypart).wait_recv()
        mixed[mb] = (OWN[mb, yh] + YR[mb].astype(F32)).astype(BF)

    for cp in loads_t[0]:
        cp.wait()
    ag_y(0)
    ag_own(0)
    for cp in loads_w:
        cp.wait()
    for sgn in (1, -1):
        w1x(sgn, 0)
    w0y()
    w1y(0)
    for sgn in (1, -1):
        w0x(sgn, 0, 0)
    for cp in loads_t[1]:
        cp.wait()
    ag_y(1)
    ag_partner(0)
    pack()
    ag_step(0, 1)
    w0y_wait()
    for sgn in (1, -1):
        w0x(sgn, 0, 1)
    ag_step(0, 2)
    for k, sgn in ((2, 1), (1, -1)):
        w1x_wait(sgn, 1)
        w1x(sgn, 1)
        w1y(k)
    ag_step(0, 3)
    ag_own(1)
    ag_partner(1)
    for sgn in (1, -1):
        w0x_wait(sgn, 1, 0)
        w0x(sgn, 1, 0)
    ag_step(0, 4)
    ag_step(1, 1)
    for sgn in (1, -1):
        w1x_wait(sgn, 2)
    w1y(3)
    wait_sibling(0)
    pick(0)
    ag_step(1, 2)
    for sgn in (1, -1):
        w0x_wait(sgn, 1, 1)
        w0x(sgn, 1, 1)
    ag_step(1, 3)
    spread(Q0, Q1, q1_s, q1_r)
    ag_step(1, 4)
    for rel in (0, 1):
        for sgn in (1, -1):
            w0x_wait(sgn, 2, rel)
    for k in range(4):
        w1y_wait(k)
    ffn(0, 0)
    ffn(0, 1)
    drain(("ag", 0))
    to_sib(0)
    rs_step(0, 4)
    wait_sibling(1)
    pick(1)
    rs_step(0, 3)
    spread_wait(Q0, Q1, q1_s, q1_r)
    sort()
    spread(Q2, Q3, q2_s, q2_r)
    ffn(1, 0)
    rs_step(0, 2)
    ffn(1, 1)
    drain(("ag", 1))
    rs_step(0, 1)
    to_sib(1)
    rs_step(1, 4)
    rs_step(0, 0)
    rs_step(1, 3)
    spread_wait(Q2, Q3, q2_s, q2_r)
    unpack()
    rs_end(0)
    rs_step(1, 2)
    rs_step(1, 1)
    rs_step(1, 0)
    drain("w")
    spread_drain(Q0, Q1, q1_s, q1_r)
    spread_drain(Q2, Q3, q2_s, q2_r)
    to_sib_drain(0)
    to_sib_drain(1)
    rs_end(1)
    drain("rs")


def on_device(tokens, route_ids, route_gates, expert_in, expert_out, old_plan, new_plan):
    source = jnp.argmax(old_plan[None, :] == new_plan[:, None], axis=1).astype(jnp.int32)
    hi = lax.reduce_precision(route_gates, 8, 7)
    lo = lax.reduce_precision(route_gates - hi, 8, 7)
    fill = ((0, 0), (0, 0), (0, 16 - TOPK))
    meta = jnp.concatenate(
        [
            jnp.pad(route_ids.astype(F32), fill, constant_values=-1.0),
            jnp.pad(hi, fill),
            jnp.pad(lo, fill),
            jnp.zeros((MB, TOK, 128 - 48), F32),
        ],
        axis=2,
    ).astype(BF)
    dma = pltpu.SemaphoreType.DMA
    hbm = pl.BlockSpec(memory_space=pl.ANY)
    smem = pl.BlockSpec(memory_space=pltpu.SMEM)
    vmem = pl.BlockSpec(memory_space=pltpu.VMEM)
    sems = [
        (8,),
        (MB, 2, 4, 2), (MB, 2, 4, 2), (MB,), (MB,), (MB, 16), (MB, 16),
        (2, 2, 2), (2, 2, 2), (4, 2), (4, 2), (2,), (2,), (2, 2, 2, 2), (2, 2, 2, 2),
        (MB, NZ, 2), (MB, NZ, 2), (MB, 2, 4, 2), (MB, 2, 4, 2), (MB,), (MB,),
        (NEX,), (NEX,), (NEX,), (NEX,),
    ]
    return pl.pallas_call(
        kernel,
        out_shape=(
            jax.ShapeDtypeStruct((MB, TOK, D), BF),
            jax.ShapeDtypeStruct((1, DK, 2 * F), BF),
            jax.ShapeDtypeStruct((1, F, DK), BF),
        ),
        in_specs=[hbm, hbm, hbm, hbm, smem, smem],
        out_specs=(vmem, vmem, vmem),
        scratch_shapes=[
            pltpu.VMEM((MB, NZ, NYH, NC, TOK, WIDE), BF),
            pltpu.VMEM((2, NDP, DK, 2 * F), BF),
            pltpu.VMEM((2, NDP, F, DK), BF),
            pltpu.VMEM((MB, NZ, 2, ROWS, D), BF),
            pltpu.VMEM((NZ * ROWS, F), BF),
            pltpu.VMEM((MB, NZ, NYH, NC, TOK, 256), BF),
            pltpu.VMEM((NZ, NYH, TOK, D), BF),
            pltpu.VMEM((MB, 2, 4, NYH, TOK, D), BF),
            pltpu.VMEM((MB, TOK, D), BF),
            pltpu.VMEM((MB, TOK, D), BF),
            pltpu.VMEM((MB, NYH, TOK, D), F32),
            pltpu.VMEM((NEX, 16, 768), BF),
            pltpu.VMEM((NEX, 16, 768), BF),
            pltpu.VMEM((NEX, 16, 768), BF),
            pltpu.VMEM((NEX, 16, 768), BF),
        ]
        + [dma(shape) for shape in sems],
        compiler_params=pltpu.CompilerParams(
            collective_id=0, has_side_effects=True, vmem_limit_bytes=62 * 2**20
        ),
        cost_estimate=pl.CostEstimate(
            flops=MB * 12 * 2**30, bytes_accessed=4 * 2**20, transcendentals=MB * 768 * F
        ),
    )(tokens, meta, expert_in, expert_out, old_plan, source)


def solution(mesh):
    in_specs = (
        P(None, ("dp", "expert"), None),
        P(None, ("dp", "expert"), None),
        P(None, ("dp", "expert"), None),
        P("expert", None, "dp", None),
        P("expert", None, None, "dp"),
        P(),
        P(),
    )
    out_specs = (P(None, ("dp", "expert"), None), P("expert", "dp", None), P("expert", None, "dp"))
    return jax.shard_map(
        on_device, mesh=mesh, in_specs=in_specs, out_specs=out_specs, check_vma=False
    )
```

```python
import jax
import jax.numpy as jnp
from jax import lax
from jax.experimental import pallas as pl
from jax.experimental.pallas import tpu as pltpu
from jax.sharding import PartitionSpec as P

MESH = pl.DeviceIdType.MESH
NX, NYL, NYH, NZ, NC = 4, 2, 2, 8, 2
NDP, NEX = NX * NYL, NYH * NZ * NC
MB, TOK, D, F, TOPK, CAP = 2, 64, 2048, 512, 10, 12
DK = D // NDP
GRP = NYH * NC * TOK
ROWS = NYH * NC * CAP
WIDE = D + 128
NB = 512
BF, F32 = jnp.bfloat16, jnp.float32


def kernel(
    tokens, meta, expert_in, expert_out, plan, source,
    mixed, moved_in, moved_out,
    T0, T1, WI, WO, XY, H, GT, DD, RV, YS, YR, OWN, PRE, Q0, Q1, Q2, Q3,
    ld_sem, agr_s, agr_r, agy_s, agy_r, ags_s, ags_r,
    w1x_s, w1x_r, w1y_s, w1y_r, w0y_s, w0y_r, w0x_s, w0x_r,
    sib_s, sib_r, rs_s, rs_r, rsy_s, rsy_r, cr_s, cr_r, q1_s, q1_r, q2_s, q2_r,
):
    dp, ex = lax.axis_index("dp"), lax.axis_index("expert")
    T = (T0, T1)
    x, yl = dp // NYL, dp % NYL
    yh, z, c = ex // (NZ * NC), (ex // NC) % NZ, ex % NC

    def zat(d):
        return (z + d + NZ) % NZ

    def xat(d):
        return ((x + d + NX) % NX) * NYL + yl

    def at_z(d):
        return (dp, (yh * NZ + zat(d)) * NC + c)

    def at_x(d):
        return (xat(d), ex)

    ypart = (dp, ((1 - yh) * NZ + z) * NC + c)
    sibling = (dp, (yh * NZ + z) * NC + 1 - c)
    lpart = (x * NYL + 1 - yl, ex)

    def remote(src, dst, ss, rs, dev):
        return pltpu.make_async_remote_copy(
            src_ref=src, dst_ref=dst, send_sem=ss, recv_sem=rs,
            device_id=dev, device_id_type=MESH,
        )

    sent = {}

    def go(key, cp):
        cp.start()
        sent.setdefault(key, []).append(cp)

    def drain(key):
        for cp in sent.pop(key, []):
            cp.wait_send()

    loads_t = [
        (
            pltpu.make_async_copy(tokens.at[0], T0.at[z, yh, c, :, pl.ds(0, D)], ld_sem.at[0]),
            pltpu.make_async_copy(meta, T0.at[z, yh, c, :, pl.ds(D, 128)], ld_sem.at[1]),
        ),
        (pltpu.make_async_copy(tokens.at[1], T1.at[z, yh, c], ld_sem.at[2]),),
    ]
    loads_w = []
    for s in range(2):
        loads_w.append(pltpu.make_async_copy(expert_in.at[0, s], WI.at[s, dp], ld_sem.at[4 + 2 * s]))
        loads_w.append(pltpu.make_async_copy(expert_out.at[0, s], WO.at[s, dp], ld_sem.at[5 + 2 * s]))
    for pair in loads_t:
        for cp in pair:
            cp.start()
    for cp in loads_w:
        cp.start()

    barrier = pltpu.get_barrier_semaphore()

    for dev in (at_z(1), at_z(-1), ypart, sibling, lpart, at_x(1), at_x(-1)):
        pl.semaphore_signal(barrier, inc=1, device_id=dev, device_id_type=MESH)
    pl.semaphore_wait(barrier, 7)

    sib_count = [0, 0]

    def chunk(mb, zs, ys):
        return T[mb].at[zs, ys, c]

    def to_sibling(mb, zs, ys):
        k = sib_count[mb]
        sib_count[mb] += 1
        go(("ag", mb), remote(chunk(mb, zs, ys), chunk(mb, zs, ys), ags_s.at[mb, k], ags_r.at[mb, k], sibling))

    def wait_sibling(mb):
        for k in range(NYH * NZ):
            ref = T[mb].at[0, 0, 0]
            remote(ref, ref, ags_s.at[mb, k], ags_r.at[mb, k], sibling).wait_recv()

    def ring(mb, sgn, d, rel):
        dr = 0 if sgn > 0 else 1
        if d == 3:
            ys = dr
        else:
            ys = yh if rel == 0 else 1 - yh
        ref = chunk(mb, zat(-sgn * d), ys)
        go(("ag", mb), remote(ref, ref, agr_s.at[mb, dr, d, rel], agr_r.at[mb, dr, d, rel], at_z(sgn)))

    def ring_wait(mb, sgn, d, rel):
        dr = 0 if sgn > 0 else 1
        if d == 4:
            ys = dr
        else:
            ys = yh if rel == 0 else 1 - yh
        zs = zat(-sgn * d)
        ref = chunk(mb, zs, ys)
        remote(ref, ref, agr_s.at[mb, dr, d - 1, rel], agr_r.at[mb, dr, d - 1, rel], at_z(sgn)).wait_recv()
        to_sibling(mb, zs, ys)

    def ag_y(mb):
        ref = chunk(mb, z, yh)
        go(("ag", mb), remote(ref, ref, agy_s.at[mb], agy_r.at[mb], ypart))

    def ag_own(mb):
        for sgn in (1, -1):
            ring(mb, sgn, 0, 0)
        to_sibling(mb, z, yh)

    def ag_partner(mb):
        ref = chunk(mb, z, 1 - yh)
        remote(ref, ref, agy_s.at[mb], agy_r.at[mb], ypart).wait_recv()
        for sgn in (1, -1):
            ring(mb, sgn, 0, 1)
        to_sibling(mb, z, 1 - yh)

    def ag_step(mb, d):
        for rel in (0, 1):
            for sgn in (1, -1):
                if d == 4 and rel == 1:
                    continue
                ring_wait(mb, sgn, d, rel)
                if d < 3:
                    ring(mb, sgn, d, rel)
        if d == 3:
            for sgn in (1, -1):
                ring(mb, sgn, 3, 0)

    x_first, y_first = [(1, 0)], [(0, 0), (0, 1), (1, 1)]

    def wblk(s, b, io, half=None):
        ref = WI if io == 0 else WO
        if half is None:
            return ref.at[s, b]
        rows = (DK if io == 0 else F) // 2
        return ref.at[s, b, pl.ds(half * rows, rows)]

    def wcopy(s, b, io, half, ss, rs, dev):
        ref = wblk(s, b, io, half)
        return remote(ref, ref, ss, rs, dev)

    def w1x(sgn, d):
        dr = 0 if sgn > 0 else 1
        for q, (s, io) in enumerate(x_first):
            half = None if d == 0 else dr
            go("w", wcopy(s, xat(-sgn * d), io, half, w1x_s.at[dr, d, q], w1x_r.at[dr, d, q], at_x(sgn)))

    def w1x_wait(sgn, d):
        dr = 0 if sgn > 0 else 1
        for q, (s, io) in enumerate(x_first):
            half = None if d == 1 else dr
            wcopy(s, xat(-sgn * d), io, half, w1x_s.at[dr, d - 1, q], w1x_r.at[dr, d - 1, q], at_x(sgn)).wait_recv()

    def w1y(k):
        d = (0, 1, -1, 2)[k]
        for q, (s, io) in enumerate(x_first):
            go("w", wcopy(s, xat(d), io, None, w1y_s.at[k, q], w1y_r.at[k, q], lpart))

    def w1y_wait(k):
        d = (0, 1, -1, 2)[k]
        for q, (s, io) in enumerate(x_first):
            b = ((x + d + NX) % NX) * NYL + 1 - yl
            wcopy(s, b, io, None, w1y_s.at[k, q], w1y_r.at[k, q], lpart).wait_recv()

    def w0y():
        for q, (s, io) in enumerate(y_first):
            go("w", wcopy(s, dp, io, None, w0y_s.at[q], w0y_r.at[q], lpart))

    def w0y_wait():
        for q, (s, io) in enumerate(y_first):
            wcopy(s, x * NYL + 1 - yl, io, None, w0y_s.at[q], w0y_r.at[q], lpart).wait_recv()

    def w0blk(d, rel):
        return ((x + d + NX) % NX) * NYL + (yl if rel == 0 else 1 - yl)

    def w0x(sgn, d, rel):
        dr = 0 if sgn > 0 else 1
        for q, (s, io) in enumerate(y_first):
            half = None if d == 0 else dr
            go("w", wcopy(s, w0blk(-sgn * d, rel), io, half, w0x_s.at[dr, d, rel, q], w0x_r.at[dr, d, rel, q], at_x(sgn)))

    def w0x_wait(sgn, d, rel):
        dr = 0 if sgn > 0 else 1
        for q, (s, io) in enumerate(y_first):
            half = None if d == 1 else dr
            wcopy(s, w0blk(-sgn * d, rel), io, half, w0x_s.at[dr, d - 1, rel, q], w0x_r.at[dr, d - 1, rel, q], at_x(sgn)).wait_recv()

    def pack():
        @pl.loop(0, NEX // 2)
        def _(i):
            for h in range(2):
                j = 2 * i + h
                Q0[j, :, 0:512] = WI[1, dp, pl.ds(pl.multiple_of(i * 16, 16), 16), h * 512:(h + 1) * 512]
                Q0[j, :, 512:768] = WO[1, dp, pl.ds(pl.multiple_of(j * 16, 16), 16), :]
        Q1[ex] = Q0[ex]

    def spread(src, dst, ss, rs):
        @pl.loop(1, NEX)
        def _(i):
            j = (ex + i) % NEX
            remote(src.at[j], dst.at[ex], ss.at[i], rs.at[i], (dp, j)).start()

    def spread_wait(src, dst, ss, rs):
        @pl.loop(1, NEX)
        def _(i):
            j = (ex - i + NEX) % NEX
            remote(src.at[j], dst.at[j], ss.at[i], rs.at[i], (dp, j)).wait_recv()

    def spread_drain(src, dst, ss, rs):
        @pl.loop(1, NEX)
        def _(i):
            j = (ex + i) % NEX
            remote(src.at[j], dst.at[ex], ss.at[i], rs.at[i], (dp, j)).wait_send()

    def sort():
        @pl.loop(0, NEX)
        def _(s):
            Q2[s] = Q1[source[s]]
        Q3[ex] = Q2[ex]

    def unpack():
        @pl.loop(0, NEX // 2)
        def _(i):
            for h in range(2):
                j = 2 * i + h
                moved_in[0, pl.ds(pl.multiple_of(i * 16, 16), 16), h * 512:(h + 1) * 512] = Q3[j, :, 0:512]
                moved_out[0, pl.ds(pl.multiple_of(j * 16, 16), 16), :] = Q3[j, :, 512:768]

    def pick(mb):
        @pl.loop(0, NZ)
        def _(g):
            info = jnp.concatenate(
                [T0[g, ys, :, :, D:WIDE].reshape(GRP // 2, 128) for ys in (yh, 1 - yh)], axis=0
            ).astype(F32).T
            ids, hi, lo = (info[48 * mb + k:48 * mb + k + 16] for k in (0, 16, 32))
            names = (ex.astype(F32), (NEX + plan[ex]).astype(F32))
            masks, his, los = [], [], []
            for name in names:
                hit = ids == name
                masks.append(jnp.max(jnp.where(hit, 1.0, 0.0), axis=0, keepdims=True))
                his.append(jnp.sum(jnp.where(hit, hi, 0.0), axis=0, keepdims=True))
                los.append(jnp.sum(jnp.where(hit, lo, 0.0), axis=0, keepdims=True))
            row = lax.broadcasted_iota(jnp.int32, (16, GRP), 0)
            stacked = jnp.where(row == 0, masks[0], jnp.where(row == 1, masks[1], 0.0))
            a = lax.broadcasted_iota(jnp.int32, (GRP, GRP), 0)
            b = lax.broadcasted_iota(jnp.int32, (GRP, GRP), 1)
            before = jnp.where((a // TOK == b // TOK) & (a < b), 1.0, 0.0).astype(BF)
            rank = jnp.dot(stacked.astype(BF), before, preferred_element_type=F32)
            lane = lax.broadcasted_iota(jnp.int32, (1, GRP), 1)
            first = ((lane // TOK) * CAP).astype(F32)
            place = lax.broadcasted_iota(jnp.int32, (ROWS, GRP), 0).astype(F32)
            hot, his_, los_ = [], [], []
            for s in range(2):
                key = jnp.where(masks[s] > 0.0, rank[s:s + 1] + first, -1.0)
                at = place == key
                hot.append(jnp.where(at, 1.0, 0.0))
                his_.append(jnp.where(at, his[s], 0.0))
                los_.append(jnp.where(at, los[s], 0.0))
            back = jnp.concatenate(his_ + los_ + [jnp.zeros((256 - 4 * ROWS, GRP), F32)], axis=0).T
            GT[mb, g] = back.astype(BF).reshape(NYH, NC, TOK, 256)
            pickm = jnp.concatenate(hot, axis=0).astype(BF)
            for n in range(D // NB):
                cols = pl.ds(n * NB, NB)
                tok = jnp.concatenate(
                    [T[mb][g, ys, :, :, cols].reshape(GRP // 2, NB) for ys in (yh, 1 - yh)], axis=0
                )
                got = jnp.dot(pickm, tok, preferred_element_type=F32).astype(BF)
                XY[mb, g, :, :, cols] = got.reshape(2, ROWS, NB)

    def ffn(mb, s):
        @pl.loop(0, F // 256)
        def _(n):
            xs = XY[mb, :, s].reshape(NZ * ROWS, D)
            col = pl.multiple_of(n * 256, 256)
            gate = jnp.dot(xs, WI[s, :, :, pl.ds(col, 256)].reshape(D, 256), preferred_element_type=F32)
            up = jnp.dot(xs, WI[s, :, :, pl.ds(col + F, 256)].reshape(D, 256), preferred_element_type=F32)
            H[:, pl.ds(col, 256)] = (gate / (1.0 + jnp.exp(-gate)) * up).astype(BF)

        @pl.loop(0, NDP)
        def _(b):
            y = jnp.dot(H[...], WO[s, b], preferred_element_type=F32).astype(BF)
            XY[mb, :, s, :, pl.ds(pl.multiple_of(b * DK, DK), DK)] = y.reshape(NZ, ROWS, DK)

    def part(mb, zd, core, rels, n):
        cols = pl.ds(pl.multiple_of(n * NB, NB), NB)
        if len(rels) == 2:
            g = GT[mb, zd, :, core].reshape(NYH * TOK, 256)
        else:
            g = GT[mb, zd, rels[0], core]
        y = XY[mb, zd, :, :, cols].reshape(2 * ROWS, NB)
        both = jnp.concatenate([y, y, jnp.zeros((256 - 4 * ROWS, NB), BF)], axis=0)
        return jnp.dot(g, both, preferred_element_type=F32).reshape(len(rels), TOK, NB)

    def dref(mb, zd, rel, cols=pl.ds(0, D)):
        if mb == 0:
            return DD.at[zd, rel, :, cols]
        return T0.at[zd, rel, 0, :, cols]

    def sref(mb, zd, rel, cols=pl.ds(0, D)):
        return T[mb].at[zd, rel, 1, :, cols]

    def sib_copy(mb, i, rel, zd):
        return remote(sref(mb, zd, rel), dref(mb, zd, rel), sib_s.at[mb, i, rel], sib_r.at[mb, i, rel], sibling)

    def turn(i):
        return zat((2 * (i % 2) - 1) * (4 - (i + 1) // 2))

    def to_sib(mb, lo, hi):
        @pl.loop(lo, hi)
        def _(i):
            zd = turn(i)

            @pl.loop(0, D // NB)
            def _(n):
                cols = pl.ds(pl.multiple_of(n * NB, NB), NB)
                v = part(mb, zd, 1 - c, (0, 1), n).astype(BF)
                for rel in range(2):
                    sref(mb, zd, rel, cols)[...] = v[rel]

            for rel in range(2):
                sib_copy(mb, i, rel, zd).start()

    def to_sib_drain(mb):
        @pl.loop(0, NZ)
        def _(i):
            for rel in range(2):
                sib_copy(mb, i, rel, turn(i)).wait_send()

    def half(h):
        return pl.ds(h * (TOK // 2), TOK // 2)

    def rs_copy(mb, dr, k, rel, h, zd):
        return remote(
            dref(mb, zd, rel).at[half(h)], RV.at[mb, dr, k, rel, half(h)],
            rs_s.at[mb, dr, k, rel, h], rs_r.at[mb, dr, k, rel, h], at_z(1 if dr == 0 else -1),
        )

    def cross_slot(mb, i):
        return RV.at[mb, (0, 0, 1)[i], (0, 1, 1)[i], 1]

    def cross_copy(mb, i, h, zd):
        return remote(
            dref(mb, zd, 1).at[half(h)], cross_slot(mb, i).at[half(h)],
            cr_s.at[mb, i, h], cr_r.at[mb, i, h], ypart,
        )

    def home_copy(mb, h):
        return remote(YS.at[mb, half(h)], YR.at[mb, half(h)], rsy_s.at[mb, h], rsy_r.at[mb, h], ypart)

    def pre(slot, mb, zd, i, rel):
        sib_copy(mb, i, rel, zd).wait_recv()

        @pl.loop(0, D // NB)
        def _(n):
            cols = pl.ds(pl.multiple_of(n * NB, NB), NB)
            PRE[slot, :, cols] = part(mb, zd, c, (rel,), n)[0] + dref(mb, zd, rel, cols)[...].astype(F32)

    def put(slot, h, arrived, out):
        @pl.loop(0, D // NB)
        def _(n):
            cols = pl.ds(pl.multiple_of(n * NB, NB), NB)
            acc = PRE[slot, half(h), cols]
            for ref in arrived:
                acc = acc + ref[half(h), cols].astype(F32)
            out.at[half(h), cols][...] = acc.astype(out.dtype)

    def cross(mb, i):
        zd = turn(i)
        pre(0, mb, zd, i, 1)
        for h in (0, 1):
            put(0, h, [], dref(mb, zd, 1))
            go("rs", cross_copy(mb, i, h, zd))

    def rs_other(mb, j):
        at = [(dr, 2 * (4 - j) - 1 + dr, turn(2 * (4 - j) - 1 + dr)) for dr in (0, 1)]
        for dr, i, zd in at:
            pre(dr, mb, zd, i, 1)
        for h in (0, 1):
            for dr, i, zd in at:
                arrived = []
                if j == 1:
                    rs_copy(mb, dr, 2, 1, h, zd).wait_recv()
                    arrived.append(RV.at[mb, dr, 2, 1])
                put(dr, h, arrived, dref(mb, zd, 1))
                go("rs", rs_copy(mb, dr, 4 - j, 1, h, zd))

    def rs_far(mb):
        zd = turn(0)
        pre(0, mb, zd, 0, 0)
        for h in (0, 1):
            cross_copy(mb, 0, h, zd).wait_recv()
            put(0, h, [cross_slot(mb, 0)], dref(mb, zd, 0))
            go("rs", rs_copy(mb, h, 0, 0, h, zd))

    def rs_own(mb, j):
        at = [(dr, 2 * (4 - j) - 1 + dr, turn(2 * (4 - j) - 1 + dr)) for dr in (0, 1)]
        for dr, i, zd in at:
            pre(dr, mb, zd, i, 0)
        for turn_h in (0, 1):
            for dr, i, zd in at:
                h = turn_h if dr == 1 else 1 - turn_h
                arrived = []
                if j == 3:
                    cross_copy(mb, i, h, zd).wait_recv()
                    arrived.append(cross_slot(mb, i))
                if j < 3 or h == dr:
                    rs_copy(mb, dr, 3 - j, 0, h, zd).wait_recv()
                    arrived.append(RV.at[mb, dr, 3 - j, 0])
                put(dr, h, arrived, dref(mb, zd, 0))
                go("rs", rs_copy(mb, dr, 4 - j, 0, h, zd))

    def rs_home(mb):
        for rel in (1, 0):
            pre(rel, mb, z, 7, rel)
        for rel in (1, 0):
            for h in (0, 1):
                for arm in (0, 1):
                    rs_copy(mb, arm, 3, rel, h, z).wait_recv()
                put(rel, h, [RV.at[mb, arm, 3, rel] for arm in (0, 1)], (OWN if rel == 0 else YS).at[mb])
                if rel == 1:
                    go("rs", home_copy(mb, h))

    def rs_end(mb):
        for h in (0, 1):
            home_copy(mb, h).wait_recv()
            mixed[mb, half(h)] = (OWN[mb, half(h)] + YR[mb, half(h)].astype(F32)).astype(BF)

    for cp in loads_t[0]:
        cp.wait()
    ag_y(0)
    ag_own(0)
    for cp in loads_w:
        cp.wait()
    for sgn in (1, -1):
        w1x(sgn, 0)
    w0y()
    w1y(0)
    for sgn in (1, -1):
        w0x(sgn, 0, 0)
    for cp in loads_t[1]:
        cp.wait()
    ag_y(1)
    ag_partner(0)
    pack()
    ag_step(0, 1)
    w0y_wait()
    for sgn in (1, -1):
        w0x(sgn, 0, 1)
    ag_step(0, 2)
    for k, sgn in ((2, 1), (1, -1)):
        w1x_wait(sgn, 1)
        w1x(sgn, 1)
        w1y(k)
    ag_step(0, 3)
    ag_own(1)
    ag_partner(1)
    for sgn in (1, -1):
        w0x_wait(sgn, 1, 0)
        w0x(sgn, 1, 0)
    ag_step(0, 4)
    ag_step(1, 1)
    for sgn in (1, -1):
        w1x_wait(sgn, 2)
    w1y(3)
    wait_sibling(0)
    pick(0)
    ag_step(1, 2)
    for sgn in (1, -1):
        w0x_wait(sgn, 1, 1)
        w0x(sgn, 1, 1)
    ag_step(1, 3)
    spread(Q0, Q1, q1_s, q1_r)
    ag_step(1, 4)
    for rel in (0, 1):
        for sgn in (1, -1):
            w0x_wait(sgn, 2, rel)
    for k in range(4):
        w1y_wait(k)
    ffn(0, 0)
    ffn(0, 1)
    drain(("ag", 0))
    def rs_first(mb):
        to_sib(mb, 0, 1)
        cross(mb, 0)
        to_sib(mb, 1, 3)
        cross(mb, 1)
        cross(mb, 2)
        to_sib(mb, 3, 5)
        rs_other(mb, 2)
        rs_far(mb)

    def rs_second(mb):
        to_sib(mb, 5, 7)
        rs_other(mb, 1)
        rs_own(mb, 3)

    rs_first(0)
    wait_sibling(1)
    pick(1)
    rs_second(0)
    spread_wait(Q0, Q1, q1_s, q1_r)
    sort()
    spread(Q2, Q3, q2_s, q2_r)
    ffn(1, 0)
    ffn(1, 1)
    rs_own(0, 2)
    drain(("ag", 1))
    rs_first(1)
    to_sib(0, 7, 8)
    rs_own(0, 1)
    rs_second(1)
    rs_home(0)
    rs_own(1, 2)
    rs_end(0)
    to_sib(1, 7, 8)
    rs_own(1, 1)
    spread_wait(Q2, Q3, q2_s, q2_r)
    unpack()
    rs_home(1)
    drain("w")
    spread_drain(Q0, Q1, q1_s, q1_r)
    spread_drain(Q2, Q3, q2_s, q2_r)
    to_sib_drain(0)
    to_sib_drain(1)
    rs_end(1)
    drain("rs")


def on_device(tokens, route_ids, route_gates, expert_in, expert_out, old_plan, new_plan):
    source = jnp.argmax(old_plan[None, :] == new_plan[:, None], axis=1).astype(jnp.int32)
    hi = lax.reduce_precision(route_gates, 8, 7)
    lo = lax.reduce_precision(route_gates - hi, 8, 7)
    fill = ((0, 0), (0, 16 - TOPK))
    parts = []
    for mb in range(MB):
        parts.append(jnp.pad(route_ids[mb].astype(F32), fill, constant_values=-1.0))
        parts.append(jnp.pad(hi[mb], fill))
        parts.append(jnp.pad(lo[mb], fill))
    parts.append(jnp.zeros((TOK, 128 - 48 * MB), F32))
    meta = jnp.concatenate(parts, axis=1).astype(BF)
    dma = pltpu.SemaphoreType.DMA
    hbm = pl.BlockSpec(memory_space=pl.ANY)
    smem = pl.BlockSpec(memory_space=pltpu.SMEM)
    vmem = pl.BlockSpec(memory_space=pltpu.VMEM)
    sems = [
        (8,),
        (MB, 2, 4, 2), (MB, 2, 4, 2), (MB,), (MB,), (MB, 16), (MB, 16),
        (2, 2, 1), (2, 2, 1), (4, 1), (4, 1), (3,), (3,), (2, 2, 2, 3), (2, 2, 2, 3),
        (MB, NZ, 2), (MB, NZ, 2), (MB, 2, 4, 2, 2), (MB, 2, 4, 2, 2), (MB, 2), (MB, 2), (MB, 3, 2), (MB, 3, 2),
        (NEX,), (NEX,), (NEX,), (NEX,),
    ]
    return pl.pallas_call(
        kernel,
        out_shape=(
            jax.ShapeDtypeStruct((MB, TOK, D), BF),
            jax.ShapeDtypeStruct((1, DK, 2 * F), BF),
            jax.ShapeDtypeStruct((1, F, DK), BF),
        ),
        in_specs=[hbm, hbm, hbm, hbm, smem, smem],
        out_specs=(vmem, vmem, vmem),
        scratch_shapes=[
            pltpu.VMEM((NZ, NYH, NC, TOK, WIDE), BF),
            pltpu.VMEM((NZ, NYH, NC, TOK, D), BF),
            pltpu.VMEM((2, NDP, DK, 2 * F), BF),
            pltpu.VMEM((2, NDP, F, DK), BF),
            pltpu.VMEM((MB, NZ, 2, ROWS, D), BF),
            pltpu.VMEM((NZ * ROWS, F), BF),
            pltpu.VMEM((MB, NZ, NYH, NC, TOK, 256), BF),
            pltpu.VMEM((NZ, NYH, TOK, D), BF),
            pltpu.VMEM((MB, 2, 4, NYH, TOK, D), BF),
            pltpu.VMEM((MB, TOK, D), BF),
            pltpu.VMEM((MB, TOK, D), BF),
            pltpu.VMEM((MB, TOK, D), F32),
            pltpu.VMEM((2, TOK, D), F32),
            pltpu.VMEM((NEX, 16, 768), BF),
            pltpu.VMEM((NEX, 16, 768), BF),
            pltpu.VMEM((NEX, 16, 768), BF),
            pltpu.VMEM((NEX, 16, 768), BF),
        ]
        + [dma(shape) for shape in sems],
        compiler_params=pltpu.CompilerParams(
            collective_id=0, has_side_effects=True, vmem_limit_bytes=62 * 2**20
        ),
        cost_estimate=pl.CostEstimate(
            flops=MB * 12 * 2**30, bytes_accessed=4 * 2**20, transcendentals=MB * 768 * F
        ),
    )(tokens, meta, expert_in, expert_out, old_plan, source)


def solution(mesh):
    in_specs = (
        P(None, ("dp", "expert"), None),
        P(None, ("dp", "expert"), None),
        P(None, ("dp", "expert"), None),
        P("expert", None, "dp", None),
        P("expert", None, None, "dp"),
        P(),
        P(),
    )
    out_specs = (P(None, ("dp", "expert"), None), P("expert", "dp", None), P("expert", None, "dp"))
    return jax.shard_map(
        on_device, mesh=mesh, in_specs=in_specs, out_specs=out_specs, check_vma=False
    )
```

```python
import jax
import jax.numpy as jnp
from jax import lax
from jax.experimental import pallas as pl
from jax.experimental.pallas import tpu as pltpu
from jax.sharding import PartitionSpec as P

MESH = pl.DeviceIdType.MESH
NX, NYL, NYH, NZ, NC = 4, 2, 2, 8, 2
NDP, NEX = NX * NYL, NYH * NZ * NC
MB, TOK, D, F, TOPK, CAP = 2, 64, 2048, 512, 10, 12
DK = D // NDP
GRP = NYH * NC * TOK
ROWS = NYH * NC * CAP
WIDE = D + 128
NB = 512
PZ = 4
BF, F32 = jnp.bfloat16, jnp.float32


def kernel(
    tokens, route_ids, route_gates, expert_in, expert_out, plan, new_plan,
    mixed, moved_in, moved_out,
    T0, T1, WI, WO, XY, H, GT, DD, RV, YS, YR, OWN, PRE, Q0, Q1, Q2, Q3, source,
    ld_sem, agr_s, agr_r, agy_s, agy_r, ags_s, ags_r,
    w1x_s, w1x_r, w1y_s, w1y_r, w0y_s, w0y_r, w0x_s, w0x_r,
    sib_s, sib_r, rs_s, rs_r, rsy_s, rsy_r, cr_s, cr_r, q1_s, q1_r, q2_s, q2_r,
):
    dp, ex = lax.axis_index("dp"), lax.axis_index("expert")
    T = (T0, T1)
    x, yl = dp // NYL, dp % NYL
    yh, z, c = ex // (NZ * NC), (ex // NC) % NZ, ex % NC

    def zat(d):
        return (z + d + NZ) % NZ

    def xat(d):
        return ((x + d + NX) % NX) * NYL + yl

    def at_z(d):
        return (dp, (yh * NZ + zat(d)) * NC + c)

    def at_x(d):
        return (xat(d), ex)

    ypart = (dp, ((1 - yh) * NZ + z) * NC + c)
    sibling = (dp, (yh * NZ + z) * NC + 1 - c)
    lpart = (x * NYL + 1 - yl, ex)

    def remote(src, dst, ss, rs, dev):
        return pltpu.make_async_remote_copy(
            src_ref=src, dst_ref=dst, send_sem=ss, recv_sem=rs,
            device_id=dev, device_id_type=MESH,
        )

    sent = {}

    def go(key, cp):
        cp.start()
        sent.setdefault(key, []).append(cp)

    def drain(key):
        for cp in sent.pop(key, []):
            cp.wait_send()

    loads_t = [
        (pltpu.make_async_copy(tokens.at[0], T0.at[z, yh, c, :, pl.ds(0, D)], ld_sem.at[0]),),
        (pltpu.make_async_copy(tokens.at[1], T1.at[z, yh, c], ld_sem.at[2]),),
    ]
    loads_w = []
    for s in range(2):
        loads_w.append(pltpu.make_async_copy(expert_in.at[0, s], WI.at[s, dp], ld_sem.at[4 + 2 * s]))
        loads_w.append(pltpu.make_async_copy(expert_out.at[0, s], WO.at[s, dp], ld_sem.at[5 + 2 * s]))
    for pair in loads_t:
        for cp in pair:
            cp.start()
    for cp in loads_w:
        cp.start()

    barrier = pltpu.get_barrier_semaphore()

    for dev in (at_z(1), at_z(-1), ypart, sibling, lpart, at_x(1), at_x(-1)):
        pl.semaphore_signal(barrier, inc=1, device_id=dev, device_id_type=MESH)

    T0[z, yh, c, :, D:WIDE] = jnp.full((TOK, WIDE - D), -1.0, BF)
    for mb in range(MB):
        hi = route_gates[mb].astype(BF)
        lo = (route_gates[mb] - hi.astype(F32)).astype(BF)
        for k, v in enumerate((route_ids[mb].astype(F32).astype(BF), hi, lo)):
            at = D + 48 * mb + 16 * k
            T0[z, yh, c, :, at:at + TOPK] = v
    pl.semaphore_wait(barrier, 7)

    sib_count = [0, 0]

    def chunk(mb, zs, ys):
        return T[mb].at[zs, ys, c]

    def to_sibling(mb, zs, ys):
        k = sib_count[mb]
        sib_count[mb] += 1
        go(("ag", mb), remote(chunk(mb, zs, ys), chunk(mb, zs, ys), ags_s.at[mb, k], ags_r.at[mb, k], sibling))

    def wait_sibling(mb):
        for k in range(NYH * NZ):
            ref = T[mb].at[0, 0, 0]
            remote(ref, ref, ags_s.at[mb, k], ags_r.at[mb, k], sibling).wait_recv()

    def ring_copy(mb, sgn, d, rel, hop):
        dr = 0 if sgn > 0 else 1
        ref = chunk(mb, zat(-sgn * (d + hop)), yh if rel == 0 else 1 - yh)
        if d == 3:
            ref = ref.at[pl.ds(dr * (TOK // 2), TOK // 2)]
        return remote(ref, ref, agr_s.at[mb, dr, d, rel], agr_r.at[mb, dr, d, rel], at_z(sgn))

    def ring(mb, sgn, d, rel):
        go(("ag", mb), ring_copy(mb, sgn, d, rel, 0))

    def cross_over(mb, k, zs, ys):
        ref = chunk(mb, zs, ys)
        return remote(ref, ref, agy_s.at[mb, k], agy_r.at[mb, k], ypart)

    def ag_y(mb):
        go(("ag", mb), cross_over(mb, 0, z, yh))

    def ag_own(mb):
        for sgn in (1, -1):
            ring(mb, sgn, 0, 0)
        to_sibling(mb, z, yh)

    def ag_partner(mb):
        cross_over(mb, 0, z, 1 - yh).wait_recv()
        for sgn in (1, -1):
            ring(mb, sgn, 0, 1)
        to_sibling(mb, z, 1 - yh)

    def ag_step(mb, d):
        for rel in (0, 1):
            for sgn in (1, -1):
                if rel == 1 and d > PZ:
                    continue
                zs = zat(-sgn * d)
                ring_copy(mb, sgn, d - 1, rel, 1).wait_recv()
                if d < (4 if rel == 0 else PZ):
                    ring(mb, sgn, d, rel)
                if d < 4:
                    to_sibling(mb, zs, yh if rel == 0 else 1 - yh)
                if PZ < d < 4:
                    go(("ag", mb), cross_over(mb, 1 if sgn > 0 else 2, zs, yh))
        if d == 4:
            to_sibling(mb, zat(4), yh)
            if PZ == 4:
                to_sibling(mb, zat(4), 1 - yh)
            else:
                go(("ag", mb), cross_over(mb, 3, zat(4), yh))

    def ag_land(mb):
        for k, d in ((1, -3), (2, 3), (3, 4)):
            if abs(d) > PZ:
                cross_over(mb, k, zat(d), 1 - yh).wait_recv()
                to_sibling(mb, zat(d), 1 - yh)

    x_first, y_first = [(1, 0)], [(0, 0), (0, 1), (1, 1)]

    def wblk(s, b, io, half=None):
        ref = WI if io == 0 else WO
        if half is None:
            return ref.at[s, b]
        rows = (DK if io == 0 else F) // 2
        return ref.at[s, b, pl.ds(half * rows, rows)]

    def wcopy(s, b, io, half, ss, rs, dev):
        ref = wblk(s, b, io, half)
        return remote(ref, ref, ss, rs, dev)

    def w1x(sgn, d):
        dr = 0 if sgn > 0 else 1
        for q, (s, io) in enumerate(x_first):
            half = None if d == 0 else dr
            go("w", wcopy(s, xat(-sgn * d), io, half, w1x_s.at[dr, d, q], w1x_r.at[dr, d, q], at_x(sgn)))

    def w1x_wait(sgn, d):
        dr = 0 if sgn > 0 else 1
        for q, (s, io) in enumerate(x_first):
            half = None if d == 1 else dr
            wcopy(s, xat(-sgn * d), io, half, w1x_s.at[dr, d - 1, q], w1x_r.at[dr, d - 1, q], at_x(sgn)).wait_recv()

    def w1y(k):
        d = (0, 1, -1, 2)[k]
        for q, (s, io) in enumerate(x_first):
            go("w", wcopy(s, xat(d), io, None, w1y_s.at[k, q], w1y_r.at[k, q], lpart))

    def w1y_wait(k):
        d = (0, 1, -1, 2)[k]
        for q, (s, io) in enumerate(x_first):
            b = ((x + d + NX) % NX) * NYL + 1 - yl
            wcopy(s, b, io, None, w1y_s.at[k, q], w1y_r.at[k, q], lpart).wait_recv()

    def w0y():
        for q, (s, io) in enumerate(y_first):
            go("w", wcopy(s, dp, io, None, w0y_s.at[q], w0y_r.at[q], lpart))

    def w0y_wait():
        for q, (s, io) in enumerate(y_first):
            wcopy(s, x * NYL + 1 - yl, io, None, w0y_s.at[q], w0y_r.at[q], lpart).wait_recv()

    def w0blk(d, rel):
        return ((x + d + NX) % NX) * NYL + (yl if rel == 0 else 1 - yl)

    def w0x(sgn, d, rel):
        dr = 0 if sgn > 0 else 1
        for q, (s, io) in enumerate(y_first):
            half = None if d == 0 else dr
            go("w", wcopy(s, w0blk(-sgn * d, rel), io, half, w0x_s.at[dr, d, rel, q], w0x_r.at[dr, d, rel, q], at_x(sgn)))

    def w0x_wait(sgn, d, rel):
        dr = 0 if sgn > 0 else 1
        for q, (s, io) in enumerate(y_first):
            half = None if d == 1 else dr
            wcopy(s, w0blk(-sgn * d, rel), io, half, w0x_s.at[dr, d - 1, rel, q], w0x_r.at[dr, d - 1, rel, q], at_x(sgn)).wait_recv()

    def pack():
        @pl.loop(0, NEX // 2)
        def _(i):
            for h in range(2):
                j = 2 * i + h
                Q0[j, :, 0:512] = WI[1, dp, pl.ds(pl.multiple_of(i * 16, 16), 16), h * 512:(h + 1) * 512]
                Q0[j, :, 512:768] = WO[1, dp, pl.ds(pl.multiple_of(j * 16, 16), 16), :]
        Q1[ex] = Q0[ex]

        @pl.loop(0, NEX)
        def _(s):
            wanted, found = new_plan[s], jnp.int32(0)
            for r in range(1, NEX):
                found = jnp.where(plan[r] == wanted, r, found)
            source[s] = found

    def spread(src, dst, ss, rs):
        @pl.loop(1, NEX)
        def _(i):
            j = (ex + i) % NEX
            remote(src.at[j], dst.at[ex], ss.at[i], rs.at[i], (dp, j)).start()

    def spread_wait(src, dst, ss, rs):
        @pl.loop(1, NEX)
        def _(i):
            j = (ex - i + NEX) % NEX
            remote(src.at[j], dst.at[j], ss.at[i], rs.at[i], (dp, j)).wait_recv()

    def spread_drain(src, dst, ss, rs):
        @pl.loop(1, NEX)
        def _(i):
            j = (ex + i) % NEX
            remote(src.at[j], dst.at[ex], ss.at[i], rs.at[i], (dp, j)).wait_send()

    def sort():
        @pl.loop(0, NEX)
        def _(s):
            Q2[s] = Q1[source[s]]
        Q3[ex] = Q2[ex]

    def unpack():
        @pl.loop(0, NEX // 2)
        def _(i):
            for h in range(2):
                j = 2 * i + h
                moved_in[0, pl.ds(pl.multiple_of(i * 16, 16), 16), h * 512:(h + 1) * 512] = Q3[j, :, 0:512]
                moved_out[0, pl.ds(pl.multiple_of(j * 16, 16), 16), :] = Q3[j, :, 512:768]

    def pick(mb):
        @pl.loop(0, NZ)
        def _(g):
            info = jnp.concatenate(
                [T0[g, ys, :, :, D:WIDE].reshape(GRP // 2, 128) for ys in (yh, 1 - yh)], axis=0
            ).astype(F32).T
            ids, hi, lo = (info[48 * mb + k:48 * mb + k + 16] for k in (0, 16, 32))
            names = (ex.astype(F32), (NEX + plan[ex]).astype(F32))
            masks, his, los = [], [], []
            for name in names:
                hit = ids == name
                masks.append(jnp.max(jnp.where(hit, 1.0, 0.0), axis=0, keepdims=True))
                his.append(jnp.sum(jnp.where(hit, hi, 0.0), axis=0, keepdims=True))
                los.append(jnp.sum(jnp.where(hit, lo, 0.0), axis=0, keepdims=True))
            row = lax.broadcasted_iota(jnp.int32, (16, GRP), 0)
            stacked = jnp.where(row == 0, masks[0], jnp.where(row == 1, masks[1], 0.0))
            a = lax.broadcasted_iota(jnp.int32, (GRP, GRP), 0)
            b = lax.broadcasted_iota(jnp.int32, (GRP, GRP), 1)
            before = jnp.where((a // TOK == b // TOK) & (a < b), 1.0, 0.0).astype(BF)
            rank = jnp.dot(stacked.astype(BF), before, preferred_element_type=F32)
            lane = lax.broadcasted_iota(jnp.int32, (1, GRP), 1)
            first = ((lane // TOK) * CAP).astype(F32)
            place = lax.broadcasted_iota(jnp.int32, (ROWS, GRP), 0).astype(F32)
            hot, his_, los_ = [], [], []
            for s in range(2):
                key = jnp.where(masks[s] > 0.0, rank[s:s + 1] + first, -1.0)
                at = place == key
                hot.append(jnp.where(at, 1.0, 0.0))
                his_.append(jnp.where(at, his[s], 0.0))
                los_.append(jnp.where(at, los[s], 0.0))
            back = jnp.concatenate(his_ + los_ + [jnp.zeros((256 - 4 * ROWS, GRP), F32)], axis=0).T
            GT[mb, g] = back.astype(BF).reshape(NYH, NC, TOK, 256)
            pickm = jnp.concatenate(hot, axis=0).astype(BF)
            for n in range(D // NB):
                cols = pl.ds(n * NB, NB)
                tok = jnp.concatenate(
                    [T[mb][g, ys, :, :, cols].reshape(GRP // 2, NB) for ys in (yh, 1 - yh)], axis=0
                )
                got = jnp.dot(pickm, tok, preferred_element_type=F32).astype(BF)
                XY[mb, g, :, :, cols] = got.reshape(2, ROWS, NB)

    def ffn(mb, s):
        @pl.loop(0, F // 256)
        def _(n):
            xs = XY[mb, :, s].reshape(NZ * ROWS, D)
            col = pl.multiple_of(n * 256, 256)
            gate = jnp.dot(xs, WI[s, :, :, pl.ds(col, 256)].reshape(D, 256), preferred_element_type=F32)
            up = jnp.dot(xs, WI[s, :, :, pl.ds(col + F, 256)].reshape(D, 256), preferred_element_type=F32)
            H[:, pl.ds(col, 256)] = (gate / (1.0 + jnp.exp(-gate)) * up).astype(BF)

        for b in range(NDP):
            y = jnp.dot(H[...], WO[s, b], preferred_element_type=F32).astype(BF)
            XY[mb, :, s, :, b * DK:(b + 1) * DK] = y.reshape(NZ, ROWS, DK)

    def part(mb, zd, core, rels, n):
        cols = pl.ds(n * NB, NB)
        if len(rels) == 2:
            g = GT[mb, zd, :, core].reshape(NYH * TOK, 256)
        else:
            g = GT[mb, zd, rels[0], core]
        y = XY[mb, zd, :, :, cols].reshape(2 * ROWS, NB)
        both = jnp.concatenate([y, y, jnp.zeros((256 - 4 * ROWS, NB), BF)], axis=0)
        return jnp.dot(g, both, preferred_element_type=F32).reshape(len(rels), TOK, NB)

    def dref(mb, zd, rel, cols=pl.ds(0, D)):
        if mb == 0:
            return DD.at[zd, rel, :, cols]
        return T0.at[zd, rel, 0, :, cols]

    def sref(mb, zd, rel, cols=pl.ds(0, D)):
        return T[mb].at[zd, rel, 1, :, cols]

    def sib_copy(mb, i, rel, zd):
        return remote(sref(mb, zd, rel), dref(mb, zd, rel), sib_s.at[mb, i, rel], sib_r.at[mb, i, rel], sibling)

    def turn(i):
        return zat((2 * (i % 2) - 1) * (4 - (i + 1) // 2))

    def to_sib(mb, lo, hi):
        @pl.loop(lo, hi)
        def _(i):
            zd = turn(i)

            for n in range(D // NB):
                cols = pl.ds(n * NB, NB)
                v = part(mb, zd, 1 - c, (0, 1), n).astype(BF)
                for rel in range(2):
                    sref(mb, zd, rel, cols)[...] = v[rel]

            for rel in range(2):
                sib_copy(mb, i, rel, zd).start()

    def to_sib_drain(mb):
        @pl.loop(0, NZ)
        def _(i):
            for rel in range(2):
                sib_copy(mb, i, rel, turn(i)).wait_send()

    def half(h):
        return pl.ds(h * (TOK // 2), TOK // 2)

    def rs_copy(mb, dr, k, rel, h, zd):
        return remote(
            dref(mb, zd, rel).at[half(h)], RV.at[mb, dr, k, rel, half(h)],
            rs_s.at[mb, dr, k, rel, h], rs_r.at[mb, dr, k, rel, h], at_z(1 if dr == 0 else -1),
        )

    def cross_slot(mb, i):
        return RV.at[mb, (0, 0, 1, 0, 1)[i], (0, 1, 1, 2, 2)[i], 1]

    def cross_copy(mb, i, h, zd):
        return remote(
            dref(mb, zd, 1).at[half(h)], cross_slot(mb, i).at[half(h)],
            cr_s.at[mb, i, h], cr_r.at[mb, i, h], ypart,
        )

    def home_copy(mb, h):
        return remote(YS.at[mb, half(h)], YR.at[mb, half(h)], rsy_s.at[mb, h], rsy_r.at[mb, h], ypart)

    def pre(slot, mb, zd, i, rel):
        sib_copy(mb, i, rel, zd).wait_recv()

        for n in range(D // NB):
            cols = pl.ds(n * NB, NB)
            PRE[slot, :, cols] = part(mb, zd, c, (rel,), n)[0] + dref(mb, zd, rel, cols)[...].astype(F32)

    def put(slot, h, arrived, out):
        for n in range(D // NB):
            cols = pl.ds(n * NB, NB)
            acc = PRE[slot, half(h), cols]
            for ref in arrived:
                acc = acc + ref[half(h), cols].astype(F32)
            out.at[half(h), cols][...] = acc.astype(out.dtype)

    def cross(mb, i):
        zd = turn(i)
        pre(0, mb, zd, i, 1)
        for h in (0, 1):
            put(0, h, [], dref(mb, zd, 1))
            go("rs", cross_copy(mb, i, h, zd))

    def rs_other(mb):
        at = [(dr, 5 + dr, turn(5 + dr)) for dr in (0, 1)]
        for dr, i, zd in at:
            pre(dr, mb, zd, i, 1)
        for h in (0, 1):
            for dr, i, zd in at:
                put(dr, h, [], dref(mb, zd, 1))
                go("rs", rs_copy(mb, dr, 3, 1, h, zd))

    def rs_far(mb):
        zd = turn(0)
        pre(0, mb, zd, 0, 0)
        for h in (0, 1):
            cross_copy(mb, 0, h, zd).wait_recv()
            put(0, h, [cross_slot(mb, 0)], dref(mb, zd, 0))
            go("rs", rs_copy(mb, h, 0, 0, h, zd))

    def rs_own(mb, j):
        at = [(dr, 2 * (4 - j) - 1 + dr, turn(2 * (4 - j) - 1 + dr)) for dr in (0, 1)]
        for dr, i, zd in at:
            pre(dr, mb, zd, i, 0)
        for turn_h in (0, 1):
            for dr, i, zd in at:
                h = turn_h if dr == 1 else 1 - turn_h
                arrived = []
                if j >= 2:
                    cross_copy(mb, i, h, zd).wait_recv()
                    arrived.append(cross_slot(mb, i))
                if j < 3 or h == dr:
                    rs_copy(mb, dr, 3 - j, 0, h, zd).wait_recv()
                    arrived.append(RV.at[mb, dr, 3 - j, 0])
                put(dr, h, arrived, dref(mb, zd, 0))
                go("rs", rs_copy(mb, dr, 4 - j, 0, h, zd))

    def rs_home(mb):
        for rel in (1, 0):
            pre(rel, mb, z, 7, rel)
        for rel in (1, 0):
            for h in (0, 1):
                for arm in (0, 1):
                    rs_copy(mb, arm, 3, rel, h, z).wait_recv()
                put(rel, h, [RV.at[mb, arm, 3, rel] for arm in (0, 1)], (OWN if rel == 0 else YS).at[mb])
                if rel == 1:
                    go("rs", home_copy(mb, h))

    def rs_end(mb):
        for h in (0, 1):
            home_copy(mb, h).wait_recv()
            mixed[mb, half(h)] = (OWN[mb, half(h)] + YR[mb, half(h)].astype(F32)).astype(BF)

    for cp in loads_t[0]:
        cp.wait()
    ag_y(0)
    ag_own(0)
    for cp in loads_w:
        cp.wait()
    for sgn in (1, -1):
        w1x(sgn, 0)
    w0y()
    w1y(0)
    for sgn in (1, -1):
        w0x(sgn, 0, 0)
    for cp in loads_t[1]:
        cp.wait()
    ag_y(1)
    ag_partner(0)
    pack()
    ag_step(0, 1)
    w0y_wait()
    for sgn in (1, -1):
        w0x(sgn, 0, 1)
    ag_step(0, 2)
    for k, sgn in ((2, 1), (1, -1)):
        w1x_wait(sgn, 1)
        w1x(sgn, 1)
        w1y(k)
    ag_step(0, 3)
    ag_own(1)
    ag_partner(1)
    for sgn in (1, -1):
        w0x_wait(sgn, 1, 0)
        w0x(sgn, 1, 0)
    ag_step(0, 4)
    ag_step(1, 1)
    for sgn in (1, -1):
        w1x_wait(sgn, 2)
    w1y(3)
    ag_land(0)
    wait_sibling(0)
    pick(0)
    ag_step(1, 2)
    for sgn in (1, -1):
        w0x_wait(sgn, 1, 1)
        w0x(sgn, 1, 1)
    ag_step(1, 3)
    spread(Q0, Q1, q1_s, q1_r)
    ag_step(1, 4)
    for rel in (0, 1):
        for sgn in (1, -1):
            w0x_wait(sgn, 2, rel)
    for k in range(4):
        w1y_wait(k)
    ffn(0, 0)
    ffn(0, 1)
    drain(("ag", 0))
    def rs_first(mb):
        to_sib(mb, 0, 1)
        cross(mb, 0)
        to_sib(mb, 1, 3)
        cross(mb, 1)
        cross(mb, 2)
        to_sib(mb, 5, 7)
        rs_other(mb)
        rs_far(mb)
        to_sib(mb, 3, 5)
        cross(mb, 3)
        cross(mb, 4)

    def rs_second(mb):
        rs_own(mb, 3)

    rs_first(0)
    ag_land(1)
    wait_sibling(1)
    pick(1)
    rs_second(0)
    spread_wait(Q0, Q1, q1_s, q1_r)
    sort()
    spread(Q2, Q3, q2_s, q2_r)
    ffn(1, 0)
    ffn(1, 1)
    rs_own(0, 2)
    drain(("ag", 1))
    rs_first(1)
    to_sib(0, 7, 8)
    rs_own(0, 1)
    rs_second(1)
    rs_home(0)
    rs_own(1, 2)
    rs_end(0)
    to_sib(1, 7, 8)
    rs_own(1, 1)
    spread_wait(Q2, Q3, q2_s, q2_r)
    unpack()
    rs_home(1)
    drain("w")
    spread_drain(Q0, Q1, q1_s, q1_r)
    spread_drain(Q2, Q3, q2_s, q2_r)
    to_sib_drain(0)
    to_sib_drain(1)
    rs_end(1)
    drain("rs")


def on_device(tokens, route_ids, route_gates, expert_in, expert_out, old_plan, new_plan):
    dma = pltpu.SemaphoreType.DMA
    hbm = pl.BlockSpec(memory_space=pl.ANY)
    smem = pl.BlockSpec(memory_space=pltpu.SMEM)
    vmem = pl.BlockSpec(memory_space=pltpu.VMEM)
    sems = [
        (8,),
        (MB, 2, 4, 2), (MB, 2, 4, 2), (MB, 4), (MB, 4), (MB, 16), (MB, 16),
        (2, 2, 1), (2, 2, 1), (4, 1), (4, 1), (3,), (3,), (2, 2, 2, 3), (2, 2, 2, 3),
        (MB, NZ, 2), (MB, NZ, 2), (MB, 2, 4, 2, 2), (MB, 2, 4, 2, 2), (MB, 2), (MB, 2), (MB, 5, 2), (MB, 5, 2),
        (NEX,), (NEX,), (NEX,), (NEX,),
    ]
    return pl.pallas_call(
        kernel,
        out_shape=(
            jax.ShapeDtypeStruct((MB, TOK, D), BF),
            jax.ShapeDtypeStruct((1, DK, 2 * F), BF),
            jax.ShapeDtypeStruct((1, F, DK), BF),
        ),
        in_specs=[hbm, vmem, vmem, hbm, hbm, smem, smem],
        out_specs=(vmem, vmem, vmem),
        scratch_shapes=[
            pltpu.VMEM((NZ, NYH, NC, TOK, WIDE), BF),
            pltpu.VMEM((NZ, NYH, NC, TOK, D), BF),
            pltpu.VMEM((2, NDP, DK, 2 * F), BF),
            pltpu.VMEM((2, NDP, F, DK), BF),
            pltpu.VMEM((MB, NZ, 2, ROWS, D), BF),
            pltpu.VMEM((NZ * ROWS, F), BF),
            pltpu.VMEM((MB, NZ, NYH, NC, TOK, 256), BF),
            pltpu.VMEM((NZ, NYH, TOK, D), BF),
            pltpu.VMEM((MB, 2, 4, NYH, TOK, D), BF),
            pltpu.VMEM((MB, TOK, D), BF),
            pltpu.VMEM((MB, TOK, D), BF),
            pltpu.VMEM((MB, TOK, D), F32),
            pltpu.VMEM((2, TOK, D), F32),
            pltpu.VMEM((NEX, 16, 768), BF),
            pltpu.VMEM((NEX, 16, 768), BF),
            pltpu.VMEM((NEX, 16, 768), BF),
            pltpu.VMEM((NEX, 16, 768), BF),
            pltpu.SMEM((NEX,), jnp.int32),
        ]
        + [dma(shape) for shape in sems],
        compiler_params=pltpu.CompilerParams(
            collective_id=0, has_side_effects=True, vmem_limit_bytes=62 * 2**20
        ),
        cost_estimate=pl.CostEstimate(
            flops=MB * 12 * 2**30, bytes_accessed=4 * 2**20, transcendentals=MB * 768 * F
        ),
    )(tokens, route_ids, route_gates, expert_in, expert_out, old_plan, new_plan)


def solution(mesh):
    in_specs = (
        P(None, ("dp", "expert"), None),
        P(None, ("dp", "expert"), None),
        P(None, ("dp", "expert"), None),
        P("expert", None, "dp", None),
        P("expert", None, None, "dp"),
        P(),
        P(),
    )
    out_specs = (P(None, ("dp", "expert"), None), P("expert", "dp", None), P("expert", None, "dp"))
    return jax.shard_map(
        on_device, mesh=mesh, in_specs=in_specs, out_specs=out_specs, check_vma=False
    )
```

```python
import jax
import jax.numpy as jnp
from jax import lax
from jax.experimental import pallas as pl
from jax.experimental.pallas import tpu as pltpu
from jax.sharding import PartitionSpec as P

MESH = pl.DeviceIdType.MESH
NX, NYL, NYH, NZ, NC = 4, 2, 2, 8, 2
NDP, NEX = NX * NYL, NYH * NZ * NC
MB, TOK, D, F, TOPK, CAP = 2, 64, 2048, 512, 10, 12
DK = D // NDP
GRP = NYH * NC * TOK
ROWS = NYH * NC * CAP
WIDE = D + 128
NB = 512
PZ = 4
BF, F32 = jnp.bfloat16, jnp.float32


def kernel(
    tokens, route_ids, route_gates, expert_in, expert_out, plan, new_plan,
    mixed, moved_in, moved_out,
    T0, T1, WI, WO, XY, H, GT, DD, RV, YS, YR, OWN, PRE, Q0, Q1, Q2, Q3, source,
    ld_sem, agr_s, agr_r, agy_s, agy_r, ags_s, ags_r,
    w1x_s, w1x_r, w1y_s, w1y_r, w0y_s, w0y_r, w0x_s, w0x_r,
    sib_s, sib_r, rs_s, rs_r, rsy_s, rsy_r, cr_s, cr_r, q1_s, q1_r, q2_s, q2_r,
):
    dp, ex = lax.axis_index("dp"), lax.axis_index("expert")
    T = (T0, T1)
    x, yl = dp // NYL, dp % NYL
    yh, z, c = ex // (NZ * NC), (ex // NC) % NZ, ex % NC

    def zat(d):
        return (z + d + NZ) % NZ

    def xat(d):
        return ((x + d + NX) % NX) * NYL + yl

    def at_z(d):
        return (dp, (yh * NZ + zat(d)) * NC + c)

    def at_x(d):
        return (xat(d), ex)

    ypart = (dp, ((1 - yh) * NZ + z) * NC + c)
    sibling = (dp, (yh * NZ + z) * NC + 1 - c)
    lpart = (x * NYL + 1 - yl, ex)

    def remote(src, dst, ss, rs, dev):
        return pltpu.make_async_remote_copy(
            src_ref=src, dst_ref=dst, send_sem=ss, recv_sem=rs,
            device_id=dev, device_id_type=MESH,
        )

    sent = {}

    def go(key, cp):
        cp.start()
        sent.setdefault(key, []).append(cp)

    def drain(key):
        for cp in sent.pop(key, []):
            cp.wait_send()

    loads_t = [
        (pltpu.make_async_copy(tokens.at[0], T0.at[z, yh, c, :, pl.ds(0, D)], ld_sem.at[0]),),
        (pltpu.make_async_copy(tokens.at[1], T1.at[z, yh, c], ld_sem.at[2]),),
    ]
    loads_w = []
    for s in range(2):
        loads_w.append(pltpu.make_async_copy(expert_in.at[0, s], WI.at[s, dp], ld_sem.at[4 + 2 * s]))
        loads_w.append(pltpu.make_async_copy(expert_out.at[0, s], WO.at[s, dp], ld_sem.at[5 + 2 * s]))
    for pair in loads_t:
        for cp in pair:
            cp.start()
    for cp in loads_w:
        cp.start()

    barrier = pltpu.get_barrier_semaphore()

    for dev in (at_z(1), at_z(-1), ypart, sibling, lpart, at_x(1), at_x(-1)):
        pl.semaphore_signal(barrier, inc=1, device_id=dev, device_id_type=MESH)

    T0[z, yh, c, :, D:WIDE] = jnp.full((TOK, WIDE - D), -1.0, BF)
    for mb in range(MB):
        hi = route_gates[mb].astype(BF)
        lo = (route_gates[mb] - hi.astype(F32)).astype(BF)
        for k, v in enumerate((route_ids[mb].astype(F32).astype(BF), hi, lo)):
            at = D + 48 * mb + 16 * k
            T0[z, yh, c, :, at:at + TOPK] = v
    pl.semaphore_wait(barrier, 7)

    sib_count = [0, 0]

    def chunk(mb, zs, ys):
        return T[mb].at[zs, ys, c]

    def to_sibling(mb, zs, ys):
        k = sib_count[mb]
        sib_count[mb] += 1
        go(("ag", mb), remote(chunk(mb, zs, ys), chunk(mb, zs, ys), ags_s.at[mb, k], ags_r.at[mb, k], sibling))

    def wait_sibling(mb):
        for k in range(NYH * NZ):
            ref = T[mb].at[0, 0, 0]
            remote(ref, ref, ags_s.at[mb, k], ags_r.at[mb, k], sibling).wait_recv()

    def ring_copy(mb, sgn, d, rel, hop):
        dr = 0 if sgn > 0 else 1
        ref = chunk(mb, zat(-sgn * (d + hop)), yh if rel == 0 else 1 - yh)
        if d == 3:
            ref = ref.at[pl.ds(dr * (TOK // 2), TOK // 2)]
        return remote(ref, ref, agr_s.at[mb, dr, d, rel], agr_r.at[mb, dr, d, rel], at_z(sgn))

    def ring(mb, sgn, d, rel):
        go(("ag", mb), ring_copy(mb, sgn, d, rel, 0))

    def cross_over(mb, k, zs, ys):
        ref = chunk(mb, zs, ys)
        return remote(ref, ref, agy_s.at[mb, k], agy_r.at[mb, k], ypart)

    def ag_y(mb):
        go(("ag", mb), cross_over(mb, 0, z, yh))

    def ag_own(mb):
        for sgn in (1, -1):
            ring(mb, sgn, 0, 0)
        to_sibling(mb, z, yh)

    def ag_partner(mb):
        cross_over(mb, 0, z, 1 - yh).wait_recv()
        for sgn in (1, -1):
            ring(mb, sgn, 0, 1)
        to_sibling(mb, z, 1 - yh)

    def ag_step(mb, d):
        for rel in (0, 1):
            for sgn in (1, -1):
                if rel == 1 and d > PZ:
                    continue
                zs = zat(-sgn * d)
                ring_copy(mb, sgn, d - 1, rel, 1).wait_recv()
                if d < (4 if rel == 0 else PZ):
                    ring(mb, sgn, d, rel)
                if d < 4:
                    to_sibling(mb, zs, yh if rel == 0 else 1 - yh)
                if PZ < d < 4:
                    go(("ag", mb), cross_over(mb, 1 if sgn > 0 else 2, zs, yh))
        if d == 4:
            to_sibling(mb, zat(4), yh)
            if PZ == 4:
                to_sibling(mb, zat(4), 1 - yh)
            else:
                go(("ag", mb), cross_over(mb, 3, zat(4), yh))

    def ag_land(mb):
        for k, d in ((1, -3), (2, 3), (3, 4)):
            if abs(d) > PZ:
                cross_over(mb, k, zat(d), 1 - yh).wait_recv()
                to_sibling(mb, zat(d), 1 - yh)

    x_first, y_first = [(1, 0)], [(0, 0), (0, 1), (1, 1)]

    def wblk(s, b, io, half=None):
        ref = WI if io == 0 else WO
        if half is None:
            return ref.at[s, b]
        rows = (DK if io == 0 else F) // 2
        return ref.at[s, b, pl.ds(half * rows, rows)]

    def wcopy(s, b, io, half, ss, rs, dev):
        ref = wblk(s, b, io, half)
        return remote(ref, ref, ss, rs, dev)

    def w1x(sgn, d):
        dr = 0 if sgn > 0 else 1
        for q, (s, io) in enumerate(x_first):
            half = None if d == 0 else dr
            go("w", wcopy(s, xat(-sgn * d), io, half, w1x_s.at[dr, d, q], w1x_r.at[dr, d, q], at_x(sgn)))

    def w1x_wait(sgn, d):
        dr = 0 if sgn > 0 else 1
        for q, (s, io) in enumerate(x_first):
            half = None if d == 1 else dr
            wcopy(s, xat(-sgn * d), io, half, w1x_s.at[dr, d - 1, q], w1x_r.at[dr, d - 1, q], at_x(sgn)).wait_recv()

    def w1y(k):
        d = (0, 1, -1, 2)[k]
        for q, (s, io) in enumerate(x_first):
            go("w", wcopy(s, xat(d), io, None, w1y_s.at[k, q], w1y_r.at[k, q], lpart))

    def w1y_wait(k):
        d = (0, 1, -1, 2)[k]
        for q, (s, io) in enumerate(x_first):
            b = ((x + d + NX) % NX) * NYL + 1 - yl
            wcopy(s, b, io, None, w1y_s.at[k, q], w1y_r.at[k, q], lpart).wait_recv()

    def w0y():
        for q, (s, io) in enumerate(y_first):
            go("w", wcopy(s, dp, io, None, w0y_s.at[q], w0y_r.at[q], lpart))

    def w0y_wait():
        for q, (s, io) in enumerate(y_first):
            wcopy(s, x * NYL + 1 - yl, io, None, w0y_s.at[q], w0y_r.at[q], lpart).wait_recv()

    def w0blk(d, rel):
        return ((x + d + NX) % NX) * NYL + (yl if rel == 0 else 1 - yl)

    def w0x(sgn, d, rel):
        dr = 0 if sgn > 0 else 1
        for q, (s, io) in enumerate(y_first):
            half = None if d == 0 else dr
            go("w", wcopy(s, w0blk(-sgn * d, rel), io, half, w0x_s.at[dr, d, rel, q], w0x_r.at[dr, d, rel, q], at_x(sgn)))

    def w0x_wait(sgn, d, rel):
        dr = 0 if sgn > 0 else 1
        for q, (s, io) in enumerate(y_first):
            half = None if d == 1 else dr
            wcopy(s, w0blk(-sgn * d, rel), io, half, w0x_s.at[dr, d - 1, rel, q], w0x_r.at[dr, d - 1, rel, q], at_x(sgn)).wait_recv()

    def pack():
        @pl.loop(0, NEX // 2)
        def _(i):
            for h in range(2):
                j = 2 * i + h
                Q0[j, :, 0:512] = WI[1, dp, pl.ds(pl.multiple_of(i * 16, 16), 16), h * 512:(h + 1) * 512]
                Q0[j, :, 512:768] = WO[1, dp, pl.ds(pl.multiple_of(j * 16, 16), 16), :]
        Q1[ex] = Q0[ex]

        @pl.loop(0, NEX)
        def _(s):
            wanted, found = new_plan[s], jnp.int32(0)
            for r in range(1, NEX):
                found = jnp.where(plan[r] == wanted, r, found)
            source[s] = found

    def spread(src, dst, ss, rs):
        @pl.loop(1, NEX)
        def _(i):
            j = (ex + i) % NEX
            remote(src.at[j], dst.at[ex], ss.at[i], rs.at[i], (dp, j)).start()

    def spread_wait(src, dst, ss, rs):
        @pl.loop(1, NEX)
        def _(i):
            j = (ex - i + NEX) % NEX
            remote(src.at[j], dst.at[j], ss.at[i], rs.at[i], (dp, j)).wait_recv()

    def spread_drain(src, dst, ss, rs):
        @pl.loop(1, NEX)
        def _(i):
            j = (ex + i) % NEX
            remote(src.at[j], dst.at[ex], ss.at[i], rs.at[i], (dp, j)).wait_send()

    def sort():
        @pl.loop(0, NEX)
        def _(s):
            Q2[s] = Q1[source[s]]
        Q3[ex] = Q2[ex]

    def unpack():
        @pl.loop(0, NEX // 2)
        def _(i):
            for h in range(2):
                j = 2 * i + h
                moved_in[0, pl.ds(pl.multiple_of(i * 16, 16), 16), h * 512:(h + 1) * 512] = Q3[j, :, 0:512]
                moved_out[0, pl.ds(pl.multiple_of(j * 16, 16), 16), :] = Q3[j, :, 512:768]

    def pick(mb):
        @pl.loop(0, NZ)
        def _(g):
            info = jnp.concatenate(
                [T0[g, ys, :, :, D:WIDE].reshape(GRP // 2, 128) for ys in (yh, 1 - yh)], axis=0
            ).astype(F32).T
            ids, hi, lo = (info[48 * mb + k:48 * mb + k + 16] for k in (0, 16, 32))
            names = (ex.astype(F32), (NEX + plan[ex]).astype(F32))
            masks, his, los = [], [], []
            for name in names:
                hit = ids == name
                masks.append(jnp.max(jnp.where(hit, 1.0, 0.0), axis=0, keepdims=True))
                his.append(jnp.sum(jnp.where(hit, hi, 0.0), axis=0, keepdims=True))
                los.append(jnp.sum(jnp.where(hit, lo, 0.0), axis=0, keepdims=True))
            row = lax.broadcasted_iota(jnp.int32, (16, GRP), 0)
            stacked = jnp.where(row == 0, masks[0], jnp.where(row == 1, masks[1], 0.0))
            a = lax.broadcasted_iota(jnp.int32, (GRP, GRP), 0)
            b = lax.broadcasted_iota(jnp.int32, (GRP, GRP), 1)
            before = jnp.where((a // TOK == b // TOK) & (a < b), 1.0, 0.0).astype(BF)
            rank = jnp.dot(stacked.astype(BF), before, preferred_element_type=F32)
            lane = lax.broadcasted_iota(jnp.int32, (1, GRP), 1)
            first = ((lane // TOK) * CAP).astype(F32)
            place = lax.broadcasted_iota(jnp.int32, (ROWS, GRP), 0).astype(F32)
            hot, his_, los_ = [], [], []
            for s in range(2):
                key = jnp.where(masks[s] > 0.0, rank[s:s + 1] + first, -1.0)
                at = place == key
                hot.append(jnp.where(at, 1.0, 0.0))
                his_.append(jnp.where(at, his[s], 0.0))
                los_.append(jnp.where(at, los[s], 0.0))
            back = jnp.concatenate(his_ + los_ + [jnp.zeros((256 - 4 * ROWS, GRP), F32)], axis=0).T
            GT[mb, g] = back.astype(BF).reshape(NYH, NC, TOK, 256)
            pickm = jnp.concatenate(hot, axis=0).astype(BF)
            for n in range(D // NB):
                cols = pl.ds(n * NB, NB)
                tok = jnp.concatenate(
                    [T[mb][g, ys, :, :, cols].reshape(GRP // 2, NB) for ys in (yh, 1 - yh)], axis=0
                )
                got = jnp.dot(pickm, tok, preferred_element_type=F32).astype(BF)
                XY[mb, g, :, :, cols] = got.reshape(2, ROWS, NB)

    def ffn(mb, s):
        @pl.loop(0, F // 256)
        def _(n):
            xs = XY[mb, :, s].reshape(NZ * ROWS, D)
            col = pl.multiple_of(n * 256, 256)
            gate = jnp.dot(xs, WI[s, :, :, pl.ds(col, 256)].reshape(D, 256), preferred_element_type=F32)
            up = jnp.dot(xs, WI[s, :, :, pl.ds(col + F, 256)].reshape(D, 256), preferred_element_type=F32)
            H[:, pl.ds(col, 256)] = (gate / (1.0 + jnp.exp(-gate)) * up).astype(BF)

        for b in range(NDP):
            y = jnp.dot(H[...], WO[s, b], preferred_element_type=F32).astype(BF)
            XY[mb, :, s, :, b * DK:(b + 1) * DK] = y.reshape(NZ, ROWS, DK)

    def part(mb, zd, core, rels, n):
        cols = pl.ds(n * NB, NB)
        if len(rels) == 2:
            g = GT[mb, zd, :, core].reshape(NYH * TOK, 256)
        else:
            g = GT[mb, zd, rels[0], core]
        y = XY[mb, zd, :, :, cols].reshape(2 * ROWS, NB)
        both = jnp.concatenate([y, y, jnp.zeros((256 - 4 * ROWS, NB), BF)], axis=0)
        return jnp.dot(g, both, preferred_element_type=F32).reshape(len(rels), TOK, NB)

    def dref(mb, zd, rel, cols=pl.ds(0, D)):
        if mb == 0:
            return DD.at[zd, rel, :, cols]
        return T0.at[zd, rel, 0, :, cols]

    def sref(mb, zd, rel, cols=pl.ds(0, D)):
        return T[mb].at[zd, rel, 1, :, cols]

    def sib_copy(mb, i, rel, zd):
        return remote(sref(mb, zd, rel), dref(mb, zd, rel), sib_s.at[mb, i, rel], sib_r.at[mb, i, rel], sibling)

    def turn(i):
        return zat((2 * (i % 2) - 1) * (4 - (i + 1) // 2))

    def to_sib(mb, lo, hi):
        @pl.loop(lo, hi)
        def _(i):
            zd = turn(i)

            for n in range(D // NB):
                cols = pl.ds(n * NB, NB)
                v = part(mb, zd, 1 - c, (0, 1), n).astype(BF)
                for rel in range(2):
                    sref(mb, zd, rel, cols)[...] = v[rel]

            for rel in range(2):
                sib_copy(mb, i, rel, zd).start()

    def to_sib_drain(mb):
        @pl.loop(0, NZ)
        def _(i):
            for rel in range(2):
                sib_copy(mb, i, rel, turn(i)).wait_send()

    def half(h):
        return pl.ds(h * (TOK // 2), TOK // 2)

    def rs_copy(mb, dr, k, rel, h, zd):
        return remote(
            dref(mb, zd, rel).at[half(h)], RV.at[mb, dr, k, rel, half(h)],
            rs_s.at[mb, dr, k, rel, h], rs_r.at[mb, dr, k, rel, h], at_z(1 if dr == 0 else -1),
        )

    def cross_slot(mb, i):
        return RV.at[mb, (0, 0, 1, 0, 1)[i], (0, 1, 1, 2, 2)[i], 1]

    def cross_copy(mb, i, h, zd):
        return remote(
            dref(mb, zd, 1).at[half(h)], cross_slot(mb, i).at[half(h)],
            cr_s.at[mb, i, h], cr_r.at[mb, i, h], ypart,
        )

    def home_copy(mb, h):
        return remote(YS.at[mb, half(h)], YR.at[mb, half(h)], rsy_s.at[mb, h], rsy_r.at[mb, h], ypart)

    def pre(slot, mb, zd, i, rel):
        sib_copy(mb, i, rel, zd).wait_recv()

        for n in range(D // NB):
            cols = pl.ds(n * NB, NB)
            PRE[slot, :, cols] = part(mb, zd, c, (rel,), n)[0] + dref(mb, zd, rel, cols)[...].astype(F32)

    def put(slot, h, arrived, out):
        for n in range(D // NB):
            cols = pl.ds(n * NB, NB)
            acc = PRE[slot, half(h), cols]
            for ref in arrived:
                acc = acc + ref[half(h), cols].astype(F32)
            out.at[half(h), cols][...] = acc.astype(out.dtype)

    def cross(mb, i):
        zd = turn(i)
        pre(0, mb, zd, i, 1)
        for h in (0, 1):
            put(0, h, [], dref(mb, zd, 1))
            go("rs", cross_copy(mb, i, h, zd))

    def rs_other(mb):
        at = [(dr, 5 + dr, turn(5 + dr)) for dr in (0, 1)]
        for dr, i, zd in at:
            pre(dr, mb, zd, i, 1)
        for h in (0, 1):
            for dr, i, zd in at:
                put(dr, h, [], dref(mb, zd, 1))
                go("rs", rs_copy(mb, dr, 3, 1, h, zd))

    def rs_far(mb):
        zd = turn(0)
        pre(0, mb, zd, 0, 0)
        for h in (0, 1):
            cross_copy(mb, 0, h, zd).wait_recv()
            put(0, h, [cross_slot(mb, 0)], dref(mb, zd, 0))
            go("rs", rs_copy(mb, h, 0, 0, h, zd))

    def rs_own(mb, j):
        at = [(dr, 2 * (4 - j) - 1 + dr, turn(2 * (4 - j) - 1 + dr)) for dr in (0, 1)]
        for dr, i, zd in at:
            pre(dr, mb, zd, i, 0)
        for turn_h in (0, 1):
            for dr, i, zd in at:
                h = turn_h if dr == 1 else 1 - turn_h
                arrived = []
                if j >= 2:
                    cross_copy(mb, i, h, zd).wait_recv()
                    arrived.append(cross_slot(mb, i))
                if j < 3 or h == dr:
                    rs_copy(mb, dr, 3 - j, 0, h, zd).wait_recv()
                    arrived.append(RV.at[mb, dr, 3 - j, 0])
                put(dr, h, arrived, dref(mb, zd, 0))
                go("rs", rs_copy(mb, dr, 4 - j, 0, h, zd))

    def rs_home(mb):
        for rel in (1, 0):
            pre(rel, mb, z, 7, rel)
        for rel in (1, 0):
            for h in (0, 1):
                for arm in (0, 1):
                    rs_copy(mb, arm, 3, rel, h, z).wait_recv()
                put(rel, h, [RV.at[mb, arm, 3, rel] for arm in (0, 1)], (OWN if rel == 0 else YS).at[mb])
                if rel == 1:
                    go("rs", home_copy(mb, h))

    def rs_end(mb):
        for h in (0, 1):
            home_copy(mb, h).wait_recv()
            mixed[mb, half(h)] = (OWN[mb, half(h)] + YR[mb, half(h)].astype(F32)).astype(BF)

    for cp in loads_t[0]:
        cp.wait()
    ag_y(0)
    ag_own(0)
    for cp in loads_w:
        cp.wait()
    w0y()
    for sgn in (1, -1):
        w1x(sgn, 0)
    for sgn in (1, -1):
        w0x(sgn, 0, 0)
    w1y(0)
    for cp in loads_t[1]:
        cp.wait()
    ag_y(1)
    ag_partner(0)
    pack()
    ag_step(0, 1)
    w0y_wait()
    for sgn in (1, -1):
        w0x(sgn, 0, 1)
    ag_step(0, 2)
    for k, sgn in ((2, 1), (1, -1)):
        w1x_wait(sgn, 1)
        w1x(sgn, 1)
        w1y(k)
    ag_step(0, 3)
    ag_own(1)
    ag_partner(1)
    for sgn in (1, -1):
        w0x_wait(sgn, 1, 0)
        w0x(sgn, 1, 0)
    ag_step(0, 4)
    ag_step(1, 1)
    for sgn in (1, -1):
        w1x_wait(sgn, 2)
    w1y(3)
    ag_land(0)
    wait_sibling(0)
    pick(0)
    ag_step(1, 2)
    for sgn in (1, -1):
        w0x_wait(sgn, 1, 1)
        w0x(sgn, 1, 1)
    ag_step(1, 3)
    spread(Q0, Q1, q1_s, q1_r)
    ag_step(1, 4)
    for rel in (0, 1):
        for sgn in (1, -1):
            w0x_wait(sgn, 2, rel)
    ffn(0, 0)
    for k in range(4):
        w1y_wait(k)
    ffn(0, 1)
    drain(("ag", 0))
    def rs_first(mb):
        to_sib(mb, 0, 1)
        cross(mb, 0)
        to_sib(mb, 1, 3)
        cross(mb, 1)
        cross(mb, 2)
        to_sib(mb, 5, 7)
        rs_other(mb)
        rs_far(mb)
        to_sib(mb, 3, 5)
        cross(mb, 3)
        cross(mb, 4)

    def rs_second(mb):
        rs_own(mb, 3)

    rs_first(0)
    ag_land(1)
    wait_sibling(1)
    pick(1)
    rs_second(0)
    spread_wait(Q0, Q1, q1_s, q1_r)
    sort()
    spread(Q2, Q3, q2_s, q2_r)
    ffn(1, 0)
    ffn(1, 1)
    drain(("ag", 1))
    rs_first(1)
    rs_own(0, 2)
    to_sib(0, 7, 8)
    rs_own(0, 1)
    rs_second(1)
    rs_home(0)
    rs_own(1, 2)
    rs_end(0)
    to_sib(1, 7, 8)
    rs_own(1, 1)
    spread_wait(Q2, Q3, q2_s, q2_r)
    unpack()
    rs_home(1)
    drain("w")
    spread_drain(Q0, Q1, q1_s, q1_r)
    spread_drain(Q2, Q3, q2_s, q2_r)
    to_sib_drain(0)
    to_sib_drain(1)
    rs_end(1)
    drain("rs")


def on_device(tokens, route_ids, route_gates, expert_in, expert_out, old_plan, new_plan):
    dma = pltpu.SemaphoreType.DMA
    hbm = pl.BlockSpec(memory_space=pl.ANY)
    smem = pl.BlockSpec(memory_space=pltpu.SMEM)
    vmem = pl.BlockSpec(memory_space=pltpu.VMEM)
    sems = [
        (8,),
        (MB, 2, 4, 2), (MB, 2, 4, 2), (MB, 4), (MB, 4), (MB, 16), (MB, 16),
        (2, 2, 1), (2, 2, 1), (4, 1), (4, 1), (3,), (3,), (2, 2, 2, 3), (2, 2, 2, 3),
        (MB, NZ, 2), (MB, NZ, 2), (MB, 2, 4, 2, 2), (MB, 2, 4, 2, 2), (MB, 2), (MB, 2), (MB, 5, 2), (MB, 5, 2),
        (NEX,), (NEX,), (NEX,), (NEX,),
    ]
    return pl.pallas_call(
        kernel,
        out_shape=(
            jax.ShapeDtypeStruct((MB, TOK, D), BF),
            jax.ShapeDtypeStruct((1, DK, 2 * F), BF),
            jax.ShapeDtypeStruct((1, F, DK), BF),
        ),
        in_specs=[hbm, vmem, vmem, hbm, hbm, smem, smem],
        out_specs=(vmem, vmem, vmem),
        scratch_shapes=[
            pltpu.VMEM((NZ, NYH, NC, TOK, WIDE), BF),
            pltpu.VMEM((NZ, NYH, NC, TOK, D), BF),
            pltpu.VMEM((2, NDP, DK, 2 * F), BF),
            pltpu.VMEM((2, NDP, F, DK), BF),
            pltpu.VMEM((MB, NZ, 2, ROWS, D), BF),
            pltpu.VMEM((NZ * ROWS, F), BF),
            pltpu.VMEM((MB, NZ, NYH, NC, TOK, 256), BF),
            pltpu.VMEM((NZ, NYH, TOK, D), BF),
            pltpu.VMEM((MB, 2, 4, NYH, TOK, D), BF),
            pltpu.VMEM((MB, TOK, D), BF),
            pltpu.VMEM((MB, TOK, D), BF),
            pltpu.VMEM((MB, TOK, D), F32),
            pltpu.VMEM((2, TOK, D), F32),
            pltpu.VMEM((NEX, 16, 768), BF),
            pltpu.VMEM((NEX, 16, 768), BF),
            pltpu.VMEM((NEX, 16, 768), BF),
            pltpu.VMEM((NEX, 16, 768), BF),
            pltpu.SMEM((NEX,), jnp.int32),
        ]
        + [dma(shape) for shape in sems],
        compiler_params=pltpu.CompilerParams(
            collective_id=0, has_side_effects=True, vmem_limit_bytes=62 * 2**20
        ),
        cost_estimate=pl.CostEstimate(
            flops=MB * 12 * 2**30, bytes_accessed=4 * 2**20, transcendentals=MB * 768 * F
        ),
    )(tokens, route_ids, route_gates, expert_in, expert_out, old_plan, new_plan)


def solution(mesh):
    in_specs = (
        P(None, ("dp", "expert"), None),
        P(None, ("dp", "expert"), None),
        P(None, ("dp", "expert"), None),
        P("expert", None, "dp", None),
        P("expert", None, None, "dp"),
        P(),
        P(),
    )
    out_specs = (P(None, ("dp", "expert"), None), P("expert", "dp", None), P("expert", None, "dp"))
    return jax.shard_map(
        on_device, mesh=mesh, in_specs=in_specs, out_specs=out_specs, check_vma=False
    )
```
